256 devices in a mesh: wide: 64 (over z, x, core), narrow: 4 (over y).
Axes of the slice: x: 4, y: 4, z: 8, core: 2. Of those that a mesh axis runs over, the one named last changes fastest.
Arguments:
- tokens: bfloat16 [32768, 4096], P('wide', 'narrow'), may hold values from -6 to 6
- cotangent: bfloat16 [32768, 1024], P('wide', 'narrow'), may hold values from -6 to 6
- frozen_key_weight: bfloat16 [4096, 1024], P(None, 'narrow'), may hold values from -0.1875 to 0.1875
- adapter_down_maps: bfloat16 [512, 64, 4096], P('wide', None, 'narrow'), may hold values from -0.09375 to 0.09375
- adapter_up_maps: bfloat16 [512, 64, 1024], P('wide', None, 'narrow'), may hold values from -0.1875 to 0.1875
- previous_down_maps: bfloat16 [512, 64, 4096], P('wide', None, 'narrow'), may hold values from -0.09375 to 0.09375
- previous_up_maps: bfloat16 [512, 64, 1024], P('wide', None, 'narrow'), may hold values from -0.1875 to 0.1875
- down_fisher_diagonal: float32 [512, 64, 4096], P('wide', None, 'narrow'), may hold values from 1 to 30
- up_fisher_diagonal: float32 [512, 64, 1024], P('wide', None, 'narrow'), may hold values from 1 to 30
- token_adapter_index: int32 [32768], P('wide'), may hold values from 0 to 511, as said below
Outputs:
- layer_input_gradient: bfloat16 [32768, 4096], P('wide', 'narrow')
- down_map_gradient: float32 [512, 64, 4096], P('wide', None, 'narrow')
- up_map_gradient: float32 [512, 64, 1024], P('wide', None, 'narrow')
The draws below stay inside these ranges and needn't reach their ends.
Inputs may be any that keep to these rules, and one draw needn't show every extreme that they name: `token_adapter_index`: adapters a with equal a // 8 share one owner. In every aligned block of 512 tokens one owner, the same in all blocks, is named by exactly 24 tokens, a second owner by exactly 10, and every other owner by at most 10.
All inputs are finite; a program needn't handle non-finite values.
Results may differ from the reference program's by a relative error of at most 0.0059.
Values may be sent and summed in bfloat16 or wider, within the bound.
A program may use at most 128 MiB of HBM per device.

```python
import math
import jax
import jax.numpy as jnp
from jax import lax

MODEL_WIDTH = 4096
KEY_OUTPUTS = 1024
ADAPTER_RANK = 64
ADAPTERS_SHARED = 8
TOK_DEV = 512
TOKENS = 32768
ADAPTER_TOTAL = 512
ROWS = 1536
N_WIDE = 64


def draw_token_adapter_index(key, part):
    key = jax.random.fold_in(key, 11)
    tenant_list = ADAPTER_TOTAL // ADAPTERS_SHARED
    blocks = TOKENS // TOK_DEV
    average = TOK_DEV // tenant_list
    busiest = 3 * average
    cold_bound = (TOK_DEV - busiest + tenant_list - 2) // (tenant_list - 1) + max(1, average // 4)
    leftover = TOK_DEV - busiest - cold_bound
    subkeys = jax.random.split(key, 4)
    hot_owner = jax.random.randint(subkeys[0], (), 0, tenant_list, dtype=jnp.int32)
    warm_owner = (hot_owner + jax.random.randint(subkeys[1], (), 1, tenant_list, dtype=jnp.int32)) % tenant_list
    low_owner = jnp.minimum(hot_owner, warm_owner)
    high_owner = jnp.maximum(hot_owner, warm_owner)
    shifts = jax.random.randint(subkeys[2], (tenant_list,), 0, ADAPTERS_SHARED, dtype=jnp.int32)
    others = jnp.arange(tenant_list - 2, dtype=jnp.int32)
    others = others + (others >= low_owner).astype(jnp.int32)
    others = others + (others >= high_owner).astype(jnp.int32)

    def one_block(block_key):
        pieces = jax.random.split(block_key, 4)
        chosen = jax.random.permutation(pieces[0], (tenant_list - 2) * cold_bound)[:leftover]
        block_owner = jnp.concatenate([jnp.full((busiest,), hot_owner, jnp.int32), jnp.full((cold_bound,), warm_owner, jnp.int32), others[chosen // cold_bound]])
        block_owner = block_owner[jax.random.permutation(pieces[1], TOK_DEV)]
        first_pick = jax.random.randint(pieces[2], (TOK_DEV,), 0, ADAPTERS_SHARED, dtype=jnp.int32)
        second_pick = jax.random.randint(pieces[3], (TOK_DEV,), 0, ADAPTERS_SHARED, dtype=jnp.int32)
        within = (jnp.minimum(first_pick, second_pick) + shifts[block_owner]) % ADAPTERS_SHARED
        return (block_owner * ADAPTERS_SHARED + within).astype(jnp.int32)
    return jax.vmap(one_block)(jax.random.split(subkeys[3], blocks)).reshape(TOKENS)


def block_scale(own_key, extent, cuts, least, top_value):
    def one(position, shards_of):
        draws = jax.random.uniform(jax.random.fold_in(jax.random.fold_in(own_key, 6), position), (shards_of,), jnp.float32, least / len(cuts), top_value / len(cuts))
        return jnp.repeat(jnp.exp(draws), extent[position] // shards_of).reshape((-1,) + (1,) * (len(extent) - position - 1))

    level = one(*cuts[0])
    for cut in cuts[1:]:
        level = level * one(*cut)
    return level


def scatter_about(key, dims, scale, most, shards=(), held_as=jnp.bfloat16):
    entries = scale * jax.random.normal(key, dims, jnp.float32)
    if shards:
        entries = entries * block_scale(key, dims, shards, -0.22, 0.18)
    return jnp.clip(entries, -most, most).astype(held_as)


def setup_inputs(seed: int = 0) -> dict:
    key_of = jax.random.split(jax.random.key(seed), 11)
    return {
        "tokens": scatter_about(key_of[0], (TOKENS, MODEL_WIDTH), 1.0, 6.0, ((0, 64), (1, 4))),
        "cotangent": scatter_about(key_of[1], (TOKENS, KEY_OUTPUTS), 1.0, 6.0, ((0, 64), (1, 4))),
        "frozen_key_weight": scatter_about(key_of[2], (MODEL_WIDTH, KEY_OUTPUTS), KEY_OUTPUTS ** -0.5, 0.1875, ((1, 4),)),
        "adapter_down_maps": scatter_about(key_of[3], (ADAPTER_TOTAL, ADAPTER_RANK, MODEL_WIDTH), MODEL_WIDTH ** -0.5, 0.09375, ((0, 64), (2, 4))),
        "adapter_up_maps": scatter_about(key_of[4], (ADAPTER_TOTAL, ADAPTER_RANK, KEY_OUTPUTS), KEY_OUTPUTS ** -0.5, 0.1875, ((0, 64), (2, 4))),
        "previous_down_maps": scatter_about(key_of[5], (ADAPTER_TOTAL, ADAPTER_RANK, MODEL_WIDTH), MODEL_WIDTH ** -0.5, 0.09375, ((0, 64), (2, 4))),
        "previous_up_maps": scatter_about(key_of[6], (ADAPTER_TOTAL, ADAPTER_RANK, KEY_OUTPUTS), KEY_OUTPUTS ** -0.5, 0.1875, ((0, 64), (2, 4))),
        "down_fisher_diagonal": jnp.clip(jnp.exp(math.log(30.0) - 3.4011974 * jax.random.uniform(key_of[7], (ADAPTER_TOTAL, ADAPTER_RANK, MODEL_WIDTH), jnp.float32) ** block_scale(key_of[7], (ADAPTER_TOTAL, ADAPTER_RANK, MODEL_WIDTH), ((0, 64), (2, 4)), -0.2, 0.2)), 1.0, 30.0),
        "up_fisher_diagonal": jnp.clip(jnp.exp(math.log(30.0) - 3.4011974 * jax.random.uniform(key_of[8], (ADAPTER_TOTAL, ADAPTER_RANK, KEY_OUTPUTS), jnp.float32) ** block_scale(key_of[8], (ADAPTER_TOTAL, ADAPTER_RANK, KEY_OUTPUTS), ((0, 64), (2, 4)), -0.2, 0.2)), 1.0, 30.0),
        "token_adapter_index": draw_token_adapter_index(jax.random.fold_in(key_of[10], 71), 0),
    }


adapter_scale = 2.0
anchor_penalty_weight = 20.0


def reference(tokens, cotangent, frozen_key_weight, adapter_down_maps, adapter_up_maps, previous_down_maps, previous_up_maps, down_fisher_diagonal, up_fisher_diagonal, token_adapter_index):
    owner_of = token_adapter_index // ADAPTERS_SHARED
    local_id = token_adapter_index % ADAPTERS_SHARED
    contract_last = (((1,), (1,)), ((), ()))
    contract_first = (((0,), (0,)), ((), ()))

    def single_tenant(loop_state, owner_now):
        chosen = owner_of == owner_now
        live_count = jnp.sum(chosen.astype(jnp.int32))
        row_index = jnp.nonzero(chosen, size=ROWS, fill_value=0)[0].astype(jnp.int32)
        is_live = jnp.arange(ROWS, dtype=jnp.int32) < live_count
        rows_x = jnp.where(is_live[:, None], tokens[row_index], jnp.zeros((), tokens.dtype))
        rows_dy = jnp.where(is_live[:, None], cotangent[row_index], jnp.zeros((), cotangent.dtype))
        row_ids = jnp.where(is_live, local_id[row_index], -1)
        offset_position = (owner_now * ADAPTERS_SHARED).astype(jnp.int32)
        flattened_down_maps = lax.dynamic_slice_in_dim(adapter_down_maps, offset_position, ADAPTERS_SHARED, 0).reshape(ADAPTERS_SHARED * ADAPTER_RANK, MODEL_WIDTH)
        flattened_up_maps = lax.dynamic_slice_in_dim(adapter_up_maps, offset_position, ADAPTERS_SHARED, 0).reshape(ADAPTERS_SHARED * ADAPTER_RANK, KEY_OUTPUTS)
        selector = (row_ids[:, None] == jnp.arange(ADAPTERS_SHARED, dtype=jnp.int32)[None, :]).astype(jnp.float32)
        u_every = lax.dot_general(rows_x, flattened_down_maps, contract_last, preferred_element_type=jnp.float32)
        g_every = lax.dot_general(rows_dy, flattened_up_maps, contract_last, preferred_element_type=jnp.float32)
        u_low = jnp.sum(u_every.reshape(ROWS, ADAPTERS_SHARED, ADAPTER_RANK) * selector[:, :, None], axis=1).astype(jnp.bfloat16)
        g_low = jnp.sum(g_every.reshape(ROWS, ADAPTERS_SHARED, ADAPTER_RANK) * selector[:, :, None], axis=1).astype(jnp.bfloat16)
        pick_mask = selector.astype(jnp.bfloat16)
        gradient_spread = (pick_mask[:, :, None] * g_low[:, None, :]).reshape(ROWS, ADAPTERS_SHARED * ADAPTER_RANK)
        u_spread = (pick_mask[:, :, None] * u_low[:, None, :]).reshape(ROWS, ADAPTERS_SHARED * ADAPTER_RANK)
        adapter_row_product = (adapter_scale * jnp.dot(gradient_spread, flattened_down_maps, preferred_element_type=jnp.float32)).astype(jnp.bfloat16)
        down_data_gradient = lax.dot_general(gradient_spread, rows_x, contract_first, preferred_element_type=jnp.float32).reshape(ADAPTERS_SHARED, ADAPTER_RANK, MODEL_WIDTH)
        up_data_gradient = lax.dot_general(u_spread, rows_dy, contract_first, preferred_element_type=jnp.float32).reshape(ADAPTERS_SHARED, ADAPTER_RANK, KEY_OUTPUTS)
        destination_index = jnp.where(is_live, row_index, TOKENS)
        loop_state = loop_state.at[destination_index].set(adapter_row_product, mode="drop")
        return loop_state, (adapter_scale * down_data_gradient, adapter_scale * up_data_gradient)

    offset_row_positions = jnp.zeros((TOKENS, MODEL_WIDTH), jnp.bfloat16)
    adapter_full_product, (down_data_gradient, up_data_gradient) = lax.scan(single_tenant, offset_row_positions, jnp.arange(N_WIDE, dtype=jnp.int32))
    down_map_gradient = down_data_gradient.reshape(ADAPTER_TOTAL, ADAPTER_RANK, MODEL_WIDTH) + anchor_penalty_weight * down_fisher_diagonal * (adapter_down_maps.astype(jnp.float32) - previous_down_maps.astype(jnp.float32))
    up_map_gradient = up_data_gradient.reshape(ADAPTER_TOTAL, ADAPTER_RANK, KEY_OUTPUTS) + anchor_penalty_weight * up_fisher_diagonal * (adapter_up_maps.astype(jnp.float32) - previous_up_maps.astype(jnp.float32))
    frozen_contribution = lax.dot_general(cotangent, frozen_key_weight, (((1,), (1,)), ((), ())), preferred_element_type=jnp.float32)
    layer_input_gradient = (frozen_contribution + adapter_full_product.astype(jnp.float32)).astype(jnp.bfloat16)
    return layer_input_gradient, down_map_gradient, up_map_gradient
```

```python
import jax
import jax.numpy as jnp
from jax import lax
from jax.experimental import pallas as pl
from jax.experimental.pallas import tpu as pltpu
from jax.sharding import PartitionSpec as P

MESH = pl.DeviceIdType.MESH
BF = jnp.bfloat16
F32 = jnp.float32

adapter_scale = 2.0
anchor_penalty_weight = 20.0

OFFSET = (1, 7, 2, 6, 3, 5, 4, 0)
MIRROR = (1, 0, 3, 2, 5, 4, 6, 7)
OWN = 7
ZROWS = 96
ZMSG = 112
SLOTS = 24
XROWS = 2 * SLOTS
XMSG = 64
PROWS = 8 * XROWS


def iota(shape, dim):
    return lax.broadcasted_iota(jnp.int32, shape, dim)


def fiota(shape, dim):
    return iota(shape, dim).astype(F32)


def onehot(hit):
    return jnp.where(hit, 1.0, 0.0).astype(BF)


def nn(a, b):
    return jnp.dot(a, b, preferred_element_type=F32)


def nt(a, b):
    return lax.dot_general(a, b, (((1,), (1,)), ((), ())), preferred_element_type=F32)


def tn(a, b):
    return lax.dot_general(a, b, (((0,), (0,)), ((), ())), preferred_element_type=F32)


def remote(src, dst, send, recv, **where):
    return pltpu.make_async_remote_copy(
        src_ref=src, dst_ref=dst, send_sem=send, recv_sem=recv, device_id=where, device_id_type=MESH
    )


def kernel(
    idx_h, tok_h, cot_h, w_h, dn_h, up_h, pdn_h, pup_h, fd_h, fu_h,
    lig_h, dg_h, ug_h,
    idx_v, tok_v, cot_v, w_v, dn_v, up_v, pdn_v, pup_v, fd_v, fu_v,
    lig_v, dg_v, ug_v, acc,
    g_mat, gt_mat, zs_dy, zs_x, zr_dy, zr_x, zs_l, zr_l,
    p_mat, pt_mat, xs_dy, xs_x, xr_dy, xr_x, xs_l, xr_l,
    mask, spread, part, ring, low, part_u, ring_u, low_u,
    loc, zdy_s, zdy_r, zx_s, zx_r, zl_s, zl_r,
    xdy_s, xdy_r, xx_s, xx_r, xl_s, xl_r, y_s, y_r,
):
    wide = lax.axis_index("wide")
    y = lax.axis_index("narrow")
    z = wide // 8
    me = wide % 8

    def z_dev(offset):
        return lax.rem(z + offset, 8) * 8 + me

    bar = pltpu.get_barrier_semaphore()
    for k in range(1, 8):
        pl.semaphore_signal(bar, inc=1, device_id={"wide": z_dev(k)}, device_id_type=MESH)
        pl.semaphore_signal(
            bar, inc=1, device_id={"wide": z * 8 + lax.rem(me + k, 8)}, device_id_type=MESH
        )
    for k in range(1, 4):
        pl.semaphore_signal(bar, inc=1, device_id={"narrow": lax.rem(y + k, 4)}, device_id_type=MESH)

    local = [
        pltpu.make_async_copy(a, b, loc.at[i])
        for i, (a, b) in enumerate(
            [
                (idx_h, idx_v), (cot_h, cot_v.at[y]), (tok_h, tok_v), (up_h, up_v), (dn_h, dn_v),
                (w_h.at[pl.ds(pl.multiple_of(y * 1024, 1024), 1024)], w_v.at[y]),
                (pdn_h, pdn_v), (pup_h, pup_v), (fd_h, fd_v), (fu_h, fu_v),
            ]
        )
    ]
    for c in local:
        c.start()

    local[0].wait()
    hi = idx_v[...] >> 6
    code = ((idx_v[...] & 63) + 1).astype(F32)
    row = iota((8, 512), 0)
    off = jnp.where(row == 7, 0, jnp.where((row & 1) == 0, (row >> 1) + 1, 7 - (row >> 1)))
    hit = ((z + off) & 7) == hi
    rank = nn(onehot(hit), onehot(iota((512, 512), 0) < iota((512, 512), 1)))
    slot = jnp.sum(jnp.where(hit, rank + row.astype(F32) * ZROWS, 0.0), axis=0, keepdims=True)
    code16 = jnp.broadcast_to(code, (16, 512)).astype(BF)
    local[1].wait()
    for b in range(8):
        g_b = onehot(slot == fiota((ZROWS, 512), 0) + float(b * ZROWS))
        g_mat[b] = g_b
        zs_dy[b, :ZROWS, :] = nn(g_b, cot_v[y]).astype(BF)
        zs_dy[b, ZROWS:, :] = jnp.zeros((ZMSG - ZROWS, 256), BF)
        zs_dy[b, ZROWS:, :ZROWS] = nt(code16, g_b).astype(BF)

    pl.semaphore_wait(bar, 17)

    def z_copy(src, dst, send, recv, b):
        return remote(
            src.at[b], dst.at[MIRROR[b]], send.at[b], recv.at[MIRROR[b]], wide=z_dev(OFFSET[b])
        )

    def z_wait(dst, send, recv, m):
        remote(dst.at[m], dst.at[m], send.at[m], recv.at[m], wide=z_dev(1)).wait_recv()

    for b in range(7):
        z_copy(zs_dy, zr_dy, zdy_s, zdy_r, b).start()
    zr_dy[OWN] = zs_dy[OWN]
    local[2].wait()
    for b in range(7):
        zs_x[b] = nn(g_mat[b], tok_v[...]).astype(BF)
        z_copy(zs_x, zr_x, zx_s, zx_r, b).start()
    zr_x[OWN] = nn(g_mat[OWN], tok_v[...]).astype(BF)

    def x_start(src, dst, send, recv, p):
        def one(j, carry):
            d = lax.rem(me + j, 8)
            remote(
                src.at[p, d], dst.at[p, me], send.at[p, d], recv.at[p, me], wide=z * 8 + d
            ).start()
            return carry

        lax.fori_loop(1, 8, one, 0)
        dst[p, me] = src[p, me]

    def x_wait(dst, send, recv, p):
        def one(j, carry):
            d = lax.rem(me + j, 8)
            remote(
                dst.at[p, d], dst.at[p, d], send.at[p, d], recv.at[p, d], wide=z * 8 + d
            ).wait_recv()
            return carry

        lax.fori_loop(1, 8, one, 0)

    upper = onehot(iota((128, 128), 0) < iota((128, 128), 1))

    def repack_dy(p):
        packed = jnp.zeros((PROWS, 256), F32)
        for i in range(2):
            m = 2 * p + i
            if m != OWN:
                z_wait(zr_dy, zdy_s, zdy_r, m)
            codes = zr_dy[m, ZROWS:, :128]
            line = codes.astype(F32)[:8]
            o8 = fiota((8, 128), 0) * 8.0
            in_o = (line > o8) & (line < o8 + 9.0)
            place = nn(onehot(in_o), upper) + o8 * (XROWS / 8.0) + float(i * SLOTS + 1)
            place = jnp.sum(jnp.where(in_o, place, 0.0), axis=0, keepdims=True) - 1.0
            p_mat[m] = onehot(place[:, :ZROWS] == fiota((PROWS, ZROWS), 0))
            packed = packed + nn(p_mat[m], zr_dy[m, :ZROWS, :])
        xs_dy[p, :, :XROWS, :] = packed.astype(BF).reshape(8, XROWS, 256)
        for d in range(8):
            sent = jnp.zeros((16, XROWS), F32)
            for i in range(2):
                m = 2 * p + i
                sent = sent + nt(
                    zr_dy[m, ZROWS:, :ZROWS], p_mat[m, d * XROWS : (d + 1) * XROWS, :]
                )
            xs_dy[p, d, XROWS:, :] = jnp.zeros((XMSG - XROWS, 256), BF)
            xs_dy[p, d, XROWS:, :XROWS] = sent.astype(BF)
        x_start(xs_dy, xr_dy, xdy_s, xdy_r, p)

    def repack_x(p):
        for i in range(2):
            if 2 * p + i != OWN:
                z_wait(zr_x, zx_s, zx_r, 2 * p + i)
        packed = nn(p_mat[2 * p], zr_x[2 * p]) + nn(p_mat[2 * p + 1], zr_x[2 * p + 1])
        xs_x[p] = packed.astype(BF).reshape(8, XROWS, 1024)
        x_start(xs_x, xr_x, xx_s, xx_r, p)

    for p in range(4):
        repack_dy(p)

    def fold(every, p):
        kept = every * mask[p].astype(F32)
        total = (kept[:, :128] + kept[:, 128:256]) + (kept[:, 256:384] + kept[:, 384:])
        return total + pltpu.roll(total, 64, 1)

    left = iota((PROWS, 128), 1) < 64

    def dy_rows(p):
        return xr_dy[p, :, :XROWS, :].reshape(PROWS, 256)

    def sum_start(halves, source, dst, n):
        source[0:2] = jnp.where(left, halves[0], halves[2]).reshape(2, 192, 128)
        source[2:4] = jnp.where(left, halves[1], halves[3]).reshape(2, 192, 128)
        for k in range(1, 4):
            t = lax.rem(y + k, 4)
            remote(source.at[t], dst.at[y], y_s.at[n, t], y_r.at[n, y], narrow=t).start()
        dst[y] = source[y]

    def y_wait(dst, n):
        for k in range(1, 4):
            t = lax.rem(y + k, 4)
            remote(dst.at[t], dst.at[t], y_s.at[n, t], y_r.at[n, t], narrow=t).wait_recv()

    def y_share(buf, n):
        for k in range(1, 4):
            t = lax.rem(y + k, 4)
            remote(buf.at[y], buf.at[y], y_s.at[n, t], y_r.at[n, y], narrow=t).start()

    def sum_share(src, dst, n):
        y_wait(src, n)
        dst[y] = ((src[0] + src[1]) + (src[2] + src[3])).astype(BF)
        y_share(dst, n + 1)

    def spread_of(buf, p):
        first = 2 * (p % 2)
        value = buf[first : first + 2].reshape(PROWS, 128).astype(F32)
        other = pltpu.roll(value, 64, 1)
        both = jnp.where(left, value, other) if p < 2 else jnp.where(left, other, value)
        return jnp.concatenate([both.astype(BF)] * 4, axis=1) * mask[p]

    def project_dy(p):
        x_wait(xr_dy, xdy_s, xdy_r, p)
        codes = xr_dy[p, :, XROWS:, :128].reshape(128, 128)
        pick = onehot(lax.rem(iota((PROWS, 128), 0), XROWS) == iota((PROWS, 128), 1))
        seen = nt(pick, codes)
        seen = jnp.where((iota((PROWS, 128), 0) // XROWS) * 16 == iota((PROWS, 128), 1), seen, 0.0)
        seen = jnp.sum(seen, axis=1, keepdims=True)
        wanted = (iota((PROWS, 512), 1) // 64 + (1 + 8 * me)).astype(F32)
        mask[p] = onehot(seen == wanted)
        return fold(nt(dy_rows(p), up_v[...]), p)

    repack_x(0)
    local[3].wait()
    halves = [project_dy(p) for p in range(4)]
    sum_start(halves, part, ring, 0)
    repack_x(1)
    sum_share(ring, low, 0)
    for k in range(1, 4):
        t = lax.rem(y + k, 4)
        remote(cot_v.at[y], cot_v.at[y], y_s.at[4, t], y_r.at[4, y], narrow=t).start()
        remote(
            w_h.at[pl.ds(pl.multiple_of(t * 1024, 1024), 1024)],
            w_v.at[y], y_s.at[5, t], y_r.at[5, y], narrow=t,
        ).start()
    local[4].wait()
    y_wait(low, 1)
    for p in range(4):
        spread[p] = spread_of(low, p)
        xs_l[p] = (adapter_scale * nn(spread[p], dn_v[...])).astype(BF).reshape(8, XROWS, 1024)
        x_start(xs_l, xr_l, xl_s, xl_r, p)
    repack_x(2)
    repack_x(3)

    for i in range(6, 10):
        local[i].wait()

    def penalty_down(i, carry):
        at = pl.ds(pl.multiple_of(i * 64, 64), 64)
        delta = dn_v[at, :].astype(F32) - pdn_v[at, :].astype(F32)
        dg_v[at, :] = anchor_penalty_weight * fd_v[at, :] * delta
        return carry

    lax.fori_loop(0, 8, penalty_down, 0)
    ug_v[...] = anchor_penalty_weight * fu_v[...] * (up_v[...].astype(F32) - pup_v[...].astype(F32))

    hi16 = jnp.broadcast_to(hi, (16, 512)).astype(F32).astype(BF)
    eye = onehot(iota((512, 512), 0) == iota((512, 512), 1))
    hi_col = nt(eye, hi16)[:, :1]
    lane = iota((512, 128), 1)
    off = jnp.where(lane == 7, 0, jnp.where((lane & 1) == 0, (lane >> 1) + 1, 7 - (lane >> 1)))
    hit = (((z + off) & 7).astype(F32) == hi_col) & (lane < 8)
    rank = nn(onehot(iota((512, 512), 0) > iota((512, 512), 1)), onehot(hit))
    slot_col = jnp.sum(
        jnp.where(hit, rank + lane.astype(F32) * ZROWS, 0.0), axis=1, keepdims=True
    )
    for p in range(4):
        gt_mat[p] = onehot(slot_col == fiota((512, 2 * ZROWS), 1) + float(p * 2 * ZROWS))

    def unpack(p):
        for i in range(2):
            codes = zr_dy[2 * p + i, ZROWS:, :128]
            col = nt(onehot(iota((ZROWS, 128), 0) == iota((ZROWS, 128), 1)), codes)[:, :1]
            o8 = fiota((ZROWS, 128), 1) * 8.0
            in_o = (col > o8) & (col < o8 + 9.0) & (o8 < 64.0)
            place = nn(onehot(iota((ZROWS, ZROWS), 0) > iota((ZROWS, ZROWS), 1)), onehot(in_o))
            place = place + o8 * (XROWS / 8.0) + float(i * SLOTS + 1)
            place = jnp.sum(jnp.where(in_o, place, 0.0), axis=1, keepdims=True) - 1.0
            pt_mat[i * ZROWS : (i + 1) * ZROWS, :] = onehot(place == fiota((ZROWS, PROWS), 1))
        x_wait(xr_l, xl_s, xl_r, p)
        rows = nn(pt_mat[...], xr_l[p].reshape(PROWS, 1024)).astype(BF)
        for i in range(2):
            m = 2 * p + i
            if m == OWN:
                zr_l[OWN] = rows[i * ZROWS : (i + 1) * ZROWS]
            else:
                zs_l[m] = rows[i * ZROWS : (i + 1) * ZROWS]
                z_copy(zs_l, zr_l, zl_s, zl_r, m).start()

    for p in range(4):
        unpack(p)

    y_wait(cot_v, 4)
    local[5].wait()
    y_wait(w_v, 5)

    def frozen(i, carry):
        at = pl.ds(pl.multiple_of(i * 128, 128), 128)
        total = nt(cot_v[0, at, :], w_v[0])
        for j in range(1, 4):
            total = total + nt(cot_v[j, at, :], w_v[j])
        acc[at, :] = total
        return carry

    lax.fori_loop(0, 4, frozen, 0)

    halves = []
    for p in range(4):
        x_wait(xr_x, xx_s, xx_r, p)
        rows = xr_x[p].reshape(PROWS, 1024)
        halves.append(fold(nt(rows, dn_v[...]), p))
        dg_v[...] += adapter_scale * tn(spread[p], rows)
    sum_start(halves, part_u, ring_u, 2)
    dg_copy = pltpu.make_async_copy(dg_v, dg_h, loc.at[10])
    dg_copy.start()
    sum_share(ring_u, low_u, 2)
    y_wait(low_u, 3)
    for p in range(4):
        ug_v[...] += adapter_scale * tn(spread_of(low_u, p), dy_rows(p))
    ug_copy = pltpu.make_async_copy(ug_v, ug_h, loc.at[11])
    ug_copy.start()

    for p in range(4):
        for i in range(2):
            if 2 * p + i != OWN:
                z_wait(zr_l, zl_s, zl_r, 2 * p + i)
        back = zr_l[2 * p : 2 * p + 2].reshape(2 * ZROWS, 1024)
        if p < 3:
            acc[...] += nn(gt_mat[p], back)
        else:
            lig_v[...] = (acc[...] + nn(gt_mat[p], back)).astype(BF)
    lig_copy = pltpu.make_async_copy(lig_v, lig_h, loc.at[12])
    lig_copy.start()

    for b in range(7):
        z_copy(zs_dy, zr_dy, zdy_s, zdy_r, b).wait_send()
        z_copy(zs_x, zr_x, zx_s, zx_r, b).wait_send()
        z_copy(zs_l, zr_l, zl_s, zl_r, b).wait_send()

    def x_sent(src, send, recv):
        def one(n, carry):
            p, d = n // 7, lax.rem(me + 1 + lax.rem(n, 7), 8)
            remote(
                src.at[p, d], src.at[p, d], send.at[p, d], recv.at[p, d], wide=z * 8 + d
            ).wait_send()
            return carry

        lax.fori_loop(0, 28, one, 0)

    x_sent(xs_dy, xdy_s, xdy_r)
    x_sent(xs_x, xx_s, xx_r)
    x_sent(xs_l, xl_s, xl_r)
    for n, buf in enumerate((ring, low, ring_u, low_u, cot_v, w_v)):
        for k in range(1, 4):
            t = lax.rem(y + k, 4)
            remote(buf.at[t], buf.at[t], y_s.at[n, t], y_r.at[n, t], narrow=t).wait_send()
    dg_copy.wait()
    ug_copy.wait()
    lig_copy.wait()


def on_device(
    tokens,
    cotangent,
    frozen_key_weight,
    adapter_down_maps,
    adapter_up_maps,
    previous_down_maps,
    previous_up_maps,
    down_fisher_diagonal,
    up_fisher_diagonal,
    token_adapter_index,
):
    vmem = pltpu.VMEM
    dma = pltpu.SemaphoreType.DMA
    scratch = [
        vmem((1, 512), jnp.int32), vmem((512, 1024), BF), vmem((4, 512, 256), BF), vmem((4, 1024, 256), BF),
        vmem((512, 1024), BF), vmem((512, 256), BF), vmem((512, 1024), BF), vmem((512, 256), BF),
        vmem((512, 1024), F32), vmem((512, 256), F32),
        vmem((512, 1024), BF), vmem((512, 1024), F32), vmem((512, 256), F32), vmem((512, 1024), F32),
        vmem((8, ZROWS, 512), BF), vmem((4, 512, 2 * ZROWS), BF),
        vmem((8, ZMSG, 256), BF), vmem((8, ZROWS, 1024), BF),
        vmem((8, ZMSG, 256), BF), vmem((8, ZROWS, 1024), BF),
        vmem((8, ZROWS, 1024), BF), vmem((8, ZROWS, 1024), BF),
        vmem((8, PROWS, ZROWS), BF), vmem((2 * ZROWS, PROWS), BF),
        vmem((4, 8, XMSG, 256), BF), vmem((4, 8, XROWS, 1024), BF),
        vmem((4, 8, XMSG, 256), BF), vmem((4, 8, XROWS, 1024), BF),
        vmem((4, 8, XROWS, 1024), BF), vmem((4, 8, XROWS, 1024), BF),
        vmem((4, PROWS, 512), BF), vmem((4, PROWS, 512), BF),
        vmem((4, 192, 128), F32), vmem((4, 192, 128), F32), vmem((4, 192, 128), BF),
        vmem((4, 192, 128), F32), vmem((4, 192, 128), F32), vmem((4, 192, 128), BF),
        dma((13,)), dma((8,)), dma((8,)), dma((8,)), dma((8,)), dma((8,)), dma((8,)),
        dma((4, 8)), dma((4, 8)), dma((4, 8)), dma((4, 8)), dma((4, 8)), dma((4, 8)),
        dma((6, 4)), dma((6, 4)),
    ]
    flat = lambda a: a.reshape(512, -1)
    lig, dg, ug = pl.pallas_call(
        kernel,
        out_shape=(
            jax.ShapeDtypeStruct((512, 1024), BF),
            jax.ShapeDtypeStruct((512, 1024), F32),
            jax.ShapeDtypeStruct((512, 256), F32),
        ),
        in_specs=[pl.BlockSpec(memory_space=pl.ANY)] * 10,
        out_specs=[pl.BlockSpec(memory_space=pl.ANY)] * 3,
        scratch_shapes=scratch,
        compiler_params=pltpu.CompilerParams(
            collective_id=0, has_side_effects=True, vmem_limit_bytes=60 * 1024 * 1024
        ),
        cost_estimate=pl.CostEstimate(flops=12_000_000_000, bytes_accessed=12_000_000, transcendentals=0),
    )(
        token_adapter_index.reshape(1, 512),
        tokens,
        cotangent,
        frozen_key_weight,
        flat(adapter_down_maps),
        flat(adapter_up_maps),
        flat(previous_down_maps),
        flat(previous_up_maps),
        flat(down_fisher_diagonal),
        flat(up_fisher_diagonal),
    )
    return lig, dg.reshape(adapter_down_maps.shape), ug.reshape(adapter_up_maps.shape)


def solution(mesh):
    in_specs = (
        P("wide", "narrow"),
        P("wide", "narrow"),
        P(None, "narrow"),
        P("wide", None, "narrow"),
        P("wide", None, "narrow"),
        P("wide", None, "narrow"),
        P("wide", None, "narrow"),
        P("wide", None, "narrow"),
        P("wide", None, "narrow"),
        P("wide"),
    )
    out_specs = (P("wide", "narrow"), P("wide", None, "narrow"), P("wide", None, "narrow"))
    return jax.shard_map(
        on_device, mesh=mesh, in_specs=in_specs, out_specs=out_specs, check_vma=False
    )
```

```python
import jax
import jax.numpy as jnp
from jax import lax
from jax.experimental import pallas as pl
from jax.experimental.pallas import tpu as pltpu
from jax.sharding import PartitionSpec as P

MESH = pl.DeviceIdType.MESH
BF = jnp.bfloat16
F32 = jnp.float32

adapter_scale = 2.0
anchor_penalty_weight = 20.0

OFFSET = (1, 7, 2, 6, 3, 5, 4, 0)
MIRROR = (1, 0, 3, 2, 5, 4, 6, 7)
OWN = 7
ZROWS = 96
ZALL = 8 * ZROWS
SLOTS = 34
PACK = 8 * SLOTS
ROWS = 4 * PACK
HALF = 576
QUARTER = 144
COLS = 256
CHUNKS = 4


def iota(shape, dim):
    return lax.broadcasted_iota(jnp.int32, shape, dim)


def fiota(shape, dim):
    return iota(shape, dim).astype(F32)


def onehot(hit):
    return jnp.where(hit, 1.0, 0.0).astype(BF)


def nn(a, b):
    return jnp.dot(a, b, preferred_element_type=F32)


def nt(a, b):
    return lax.dot_general(a, b, (((1,), (1,)), ((), ())), preferred_element_type=F32)


def tn(a, b):
    return lax.dot_general(a, b, (((0,), (0,)), ((), ())), preferred_element_type=F32)


def remote(src, dst, send, recv, **where):
    return pltpu.make_async_remote_copy(
        src_ref=src, dst_ref=dst, send_sem=send, recv_sem=recv, device_id=where, device_id_type=MESH
    )


def offset_at(block):
    half = block >> 1
    return jnp.where(block == OWN, 0, jnp.where((block & 1) == 0, half + 1, 7 - half))


def kernel(
    idx_h, tok_h, cot_h, w_h, dn_h, up_h, pdn_h, pup_h, fd_h, fu_h,
    lig_h, dg_h, ug_h,
    idx_v, tok_v, cot_v, w_v, dn_v, up_v, pdn_v, pup_v, fd_v, fu_v,
    lig_v, dg_v, ug_v, acc,
    g_mat, gt_mat, p_mat, pt_mat,
    zs, zr, zs_c, zr_c, xs, xr, xs_c, xr_c, ls, lr, zs_l, zr_l,
    mask, spread, spread_u, part, ring, low, part_u, ring_u, low_u,
    dgs, dgr, ugs, ugr,
    loc, z_s, z_r, zc_s, zc_r, zl_s, zl_r, x_s, x_r, xc_s, xc_r, xl_s, xl_r, y_s, y_r, c_s, c_r,
):
    wide = lax.axis_index("wide")
    y = lax.axis_index("narrow")
    z = wide // 8
    me = wide % 8
    x = me // 2
    core = me % 2
    twin = wide + 1 - 2 * core

    def z_dev(offset):
        return lax.rem(z + offset, 8) * 8 + me

    def x_at(k):
        return lax.rem(x + k, 4)

    def x_dev(t):
        return z * 8 + t * 2 + core

    bar = pltpu.get_barrier_semaphore()
    for k in range(1, 8):
        pl.semaphore_signal(bar, inc=1, device_id={"wide": z_dev(k)}, device_id_type=MESH)
    for k in range(1, 4):
        pl.semaphore_signal(bar, inc=1, device_id={"wide": x_dev(x_at(k))}, device_id_type=MESH)
        pl.semaphore_signal(bar, inc=1, device_id={"narrow": lax.rem(y + k, 4)}, device_id_type=MESH)
    pl.semaphore_signal(bar, inc=1, device_id={"wide": twin}, device_id_type=MESH)

    local = [
        pltpu.make_async_copy(a, b, loc.at[i])
        for i, (a, b) in enumerate(
            [
                (idx_h, idx_v), (cot_h, cot_v.at[y]), (tok_h, tok_v), (up_h, up_v.at[core]), (dn_h, dn_v.at[core]),
                (w_h.at[pl.ds(pl.multiple_of(y * 1024, 1024), 1024)], w_v.at[y]),
                (pdn_h, pdn_v), (pup_h, pup_v), (fd_h, fd_v), (fu_h, fu_v),
            ]
        )
    ]
    for c in local:
        c.start()

    local[0].wait()
    hi = idx_v[...] >> 6
    code = ((idx_v[...] & 63) + 1).astype(F32)
    row = iota((8, 512), 0)
    hit = ((z + offset_at(row)) & 7) == hi
    rank = nn(onehot(hit), onehot(iota((512, 512), 0) < iota((512, 512), 1)))
    slot = jnp.sum(jnp.where(hit, rank + row.astype(F32) * ZROWS, 0.0), axis=0, keepdims=True)
    g_mat[...] = onehot(slot == fiota((ZALL, 512), 0))
    code16 = jnp.broadcast_to(code, (16, 512)).astype(BF)
    for b in range(8):
        sent = nt(code16, g_mat[b * ZROWS : (b + 1) * ZROWS, :])[:1]
        zs_c[b] = jnp.concatenate([sent, jnp.zeros((1, 128 - ZROWS), F32)], axis=1)
    local[1].wait()
    zs[0] = nn(g_mat[...], cot_v[y]).astype(BF).reshape(8, ZROWS, COLS)

    pl.semaphore_wait(bar, 14)

    def z_copy(src, dst, send, recv, b):
        return remote(src.at[b], dst.at[MIRROR[b]], send.at[b], recv.at[MIRROR[b]], wide=z_dev(OFFSET[b]))

    def z_start(src, dst, send, recv):
        for b in range(7):
            z_copy(src, dst, send, recv, b).start()
        dst[OWN] = src[OWN]

    def z_wait(dst, send, recv):
        for b in range(7):
            remote(dst.at[b], dst.at[b], send.at[b], recv.at[b], wide=z_dev(OFFSET[b])).wait_recv()

    def z_sent(src, send, recv):
        for b in range(7):
            remote(src.at[b], src.at[b], send.at[b], recv.at[b], wide=z_dev(OFFSET[b])).wait_send()

    def x_start(src, dst, send, recv):
        for k in range(1, 4):
            t = x_at(k)
            remote(src.at[t], dst.at[x], send.at[t], recv.at[x], wide=x_dev(t)).start()
        dst[x] = src[x]

    def x_wait(dst, send, recv):
        for k in range(1, 4):
            t = x_at(k)
            remote(dst.at[t], dst.at[t], send.at[t], recv.at[t], wide=x_dev(t)).wait_recv()

    def x_sent(src, send, recv):
        for k in range(1, 4):
            t = x_at(k)
            remote(src.at[t], src.at[t], send.at[t], recv.at[t], wide=x_dev(t)).wait_send()

    def to_twin(src, dst, n):
        return remote(src, dst, c_s.at[n], c_r.at[n], wide=twin)

    z_start(zs_c, zr_c, zc_s, zc_r)
    z_start(zs.at[0], zr.at[0], z_s.at[0], z_r.at[0])
    local[3].wait()
    local[4].wait()
    to_twin(up_v.at[core], up_v.at[core], 0).start()
    to_twin(dn_v.at[core], dn_v.at[core], 1).start()

    def y_share(buf, n):
        for k in range(1, 4):
            t = lax.rem(y + k, 4)
            remote(buf.at[y], buf.at[y], y_s.at[n, t], y_r.at[n, y], narrow=t).start()

    def y_wait(dst, n):
        for k in range(1, 4):
            t = lax.rem(y + k, 4)
            remote(dst.at[t], dst.at[t], y_s.at[n, t], y_r.at[n, t], narrow=t).wait_recv()

    y_share(cot_v, 4)
    local[2].wait()
    for k in range(CHUNKS):
        packed = nn(g_mat[...], tok_v[:, k * COLS : (k + 1) * COLS])
        zs[1 + k] = packed.astype(BF).reshape(8, ZROWS, COLS)
        z_start(zs.at[1 + k], zr.at[1 + k], z_s.at[1 + k], z_r.at[1 + k])

    z_wait(zr_c, zc_s, zc_r)
    codes = zr_c[:, 0, :]
    upper = onehot(iota((128, 128), 0) < iota((128, 128), 1))
    place = jnp.zeros((8, 128), F32)
    for t in range(4):
        inside = (codes > 16.0 * t) & (codes < 16.0 * t + 17.0)
        spot = nn(onehot(inside), upper) + fiota((8, 128), 0) * SLOTS + float(t * PACK + 1)
        place = place + jnp.where(inside, spot, 0.0)
    place = jnp.concatenate([place[m : m + 1, :ZROWS] for m in range(8)], axis=1) - 1.0
    p_mat[...] = onehot(place == fiota((ROWS, ZALL), 0))
    line = jnp.concatenate([codes[m : m + 1, :ZROWS] for m in range(8)], axis=1)
    line = jnp.broadcast_to(line, (16, ZALL)).astype(BF)
    for t in range(4):
        sent = nt(line, p_mat[t * PACK : (t + 1) * PACK, :])
        xs_c[t] = jnp.concatenate([sent, jnp.zeros((16, 384 - PACK), F32)], axis=1).astype(BF)
    x_start(xs_c, xr_c, xc_s, xc_r)

    def repack(k):
        z_wait(zr.at[k], z_s.at[k], z_r.at[k])
        xs[k] = nn(p_mat[...], zr[k].reshape(ZALL, COLS)).astype(BF).reshape(4, PACK, COLS)
        x_start(xs.at[k], xr.at[k], x_s.at[k], x_r.at[k])

    repack(0)

    codes32 = jnp.concatenate([jnp.broadcast_to(codes[m : m + 1], (4, 128)) for m in range(8)], axis=0)
    col = nt(onehot(iota((ZROWS, 128), 0) == iota((ZROWS, 128), 1)), codes32.astype(BF))
    lane = iota((ZROWS, 32), 1)
    first = (lane & 3).astype(F32) * 16.0
    inside = (col > first) & (col < first + 17.0)
    spot = nn(onehot(iota((ZROWS, ZROWS), 0) > iota((ZROWS, ZROWS), 1)), onehot(inside))
    spot = spot + ((lane & 3) * PACK + (lane >> 2) * SLOTS + 1).astype(F32)
    for m in range(8):
        at = jnp.sum(jnp.where(inside & ((lane >> 2) == m), spot, 0.0), axis=1, keepdims=True) - 1.0
        pt_mat[m * ZROWS : (m + 1) * ZROWS, :] = onehot(at == fiota((ZROWS, ROWS), 1))

    x_wait(xr_c, xc_s, xc_r)
    for t in range(4):
        seen = nt(onehot(iota((PACK, 384), 0) == iota((PACK, 384), 1)), xr_c[t])[:, :1]
        wanted = (iota((PACK, 1024), 1) // 64 + (1 + 16 * x)).astype(F32)
        mask[t] = onehot(seen == wanted)

    def fold(every, t):
        kept = every * mask[t].astype(F32)
        total = kept[:, :128]
        for j in range(1, 8):
            total = total + kept[:, j * 128 : (j + 1) * 128]
        return total + pltpu.roll(total, 64, 1)

    left = iota((HALF, 128), 1) < 64

    def sum_start(rows, source, dst, n):
        lower = jnp.concatenate([rows[HALF:], jnp.zeros((2 * HALF - ROWS, 128), F32)], axis=0)
        source[...] = jnp.where(left, rows[:HALF], lower).reshape(4, QUARTER, 128)
        for k in range(1, 4):
            t = lax.rem(y + k, 4)
            remote(source.at[t], dst.at[y], y_s.at[n, t], y_r.at[n, y], narrow=t).start()
        dst[y] = source[y]

    def sum_share(src, dst, n):
        y_wait(src, n)
        dst[y] = ((src[0] + src[1]) + (src[2] + src[3])).astype(BF)
        y_share(dst, n + 1)

    def spread_of(buf, out):
        value = buf[...].reshape(HALF, 128).astype(F32)
        other = pltpu.roll(value, 64, 1)
        high = jnp.where(left, value, other).astype(BF)
        rest = jnp.where(left, other, value).astype(BF)
        both = jnp.concatenate([high, rest[: ROWS - HALF]], axis=0)
        for t in range(4):
            one = jnp.concatenate([both[t * PACK : (t + 1) * PACK]] * 4, axis=1)
            for c in range(2):
                out[c, t * PACK : (t + 1) * PACK, :] = one * mask[t, :, c * 512 : (c + 1) * 512]

    to_twin(up_v.at[1 - core], up_v.at[1 - core], 0).wait_recv()
    x_wait(xr.at[0], x_s.at[0], x_r.at[0])
    up_all = up_v[...].reshape(1024, COLS)
    sum_start(
        jnp.concatenate([fold(nt(xr[0, t], up_all), t) for t in range(4)], axis=0), part, ring, 0
    )
    repack(1)
    sum_share(ring, low, 0)
    for k in range(1, 4):
        t = lax.rem(y + k, 4)
        remote(
            w_h.at[pl.ds(pl.multiple_of(t * 1024, 1024), 1024)],
            w_v.at[y], y_s.at[5, t], y_r.at[5, y], narrow=t,
        ).start()
    to_twin(dn_v.at[1 - core], dn_v.at[1 - core], 1).wait_recv()
    y_wait(low, 1)
    spread_of(low, spread)

    def lora(k):
        cols = slice(k * COLS, (k + 1) * COLS)
        rows = nn(spread[0], dn_v[0, :, cols]) + nn(spread[1], dn_v[1, :, cols])
        ls[k] = (adapter_scale * rows).astype(BF).reshape(4, PACK, COLS)
        x_start(ls.at[k], lr.at[k], xl_s.at[k], xl_r.at[k])

    def unpack(k):
        x_wait(lr.at[k], xl_s.at[k], xl_r.at[k])
        rows = nn(pt_mat[...], lr[k].reshape(ROWS, COLS)).astype(BF)
        zs_l[k] = rows.reshape(8, ZROWS, COLS)
        z_start(zs_l.at[k], zr_l.at[k], zl_s.at[k], zl_r.at[k])

    lora(0)
    repack(2)
    lora(1)
    lora(2)

    for i in range(6, 10):
        local[i].wait()

    def penalty_down(i, carry):
        at = pl.ds(pl.multiple_of(i * 64, 64), 64)
        delta = dn_v[core, at, :].astype(F32) - pdn_v[at, :].astype(F32)
        dg_v[at, :] = anchor_penalty_weight * fd_v[at, :] * delta
        return carry

    lax.fori_loop(0, 8, penalty_down, 0)
    delta = up_v[core].astype(F32) - pup_v[...].astype(F32)
    ug_v[...] = anchor_penalty_weight * fu_v[...] * delta

    unpack(0)
    repack(3)
    lora(3)
    unpack(1)
    repack(4)

    hi16 = jnp.broadcast_to(hi, (16, 512)).astype(F32).astype(BF)
    hi_col = nt(onehot(iota((512, 512), 0) == iota((512, 512), 1)), hi16)[:, :1]
    lane = iota((512, 128), 1)
    hit = (((z + offset_at(lane)) & 7).astype(F32) == hi_col) & (lane < 8)
    rank = nn(onehot(iota((512, 512), 0) > iota((512, 512), 1)), onehot(hit))
    slot_col = jnp.sum(jnp.where(hit, rank + lane.astype(F32) * ZROWS, 0.0), axis=1, keepdims=True)
    gt_mat[...] = onehot(slot_col == fiota((512, ZALL), 1))

    unpack(2)

    def gradient(k):
        x_wait(xr.at[k + 1], x_s.at[k + 1], x_r.at[k + 1])
        rows = xr[k + 1].reshape(ROWS, COLS)
        cols = slice(k * COLS, (k + 1) * COLS)
        dgs[k] = adapter_scale * tn(spread[1 - core], rows)
        to_twin(dgs.at[k], dgr.at[k], 2 + k).start()
        dg_v[:, cols] += adapter_scale * tn(spread[core], rows)

    gradient(0)
    gradient(1)
    unpack(3)
    gradient(2)
    gradient(3)

    def down_all(k):
        return dn_v[:, :, k * COLS : (k + 1) * COLS].reshape(1024, COLS)

    sums = []
    for t in range(4):
        every = nt(xr[1, t], down_all(0))
        for k in range(1, CHUNKS):
            every = every + nt(xr[1 + k, t], down_all(k))
        sums.append(fold(every, t))
    sum_start(jnp.concatenate(sums, axis=0), part_u, ring_u, 2)

    y_wait(cot_v, 4)
    local[5].wait()
    y_wait(w_v, 5)

    def frozen(i, carry):
        at = pl.ds(pl.multiple_of(i * 128, 128), 128)
        total = nt(cot_v[0, at, :], w_v[0])
        for j in range(1, 4):
            total = total + nt(cot_v[j, at, :], w_v[j])
        acc[at, :] = total
        return carry

    lax.fori_loop(0, 4, frozen, 0)

    sum_share(ring_u, low_u, 2)
    for k in range(CHUNKS):
        to_twin(dgr.at[k], dgr.at[k], 2 + k).wait_recv()
        dg_v[:, k * COLS : (k + 1) * COLS] += dgr[k]
    dg_copy = pltpu.make_async_copy(dg_v, dg_h, loc.at[10])
    dg_copy.start()
    y_wait(low_u, 3)
    spread_of(low_u, spread_u)
    ugs[...] = adapter_scale * tn(spread_u[1 - core], xr[0].reshape(ROWS, COLS))
    to_twin(ugs, ugr, 6).start()
    ug_v[...] += adapter_scale * tn(spread_u[core], xr[0].reshape(ROWS, COLS))

    def finish(k):
        cols = slice(k * COLS, (k + 1) * COLS)
        z_wait(zr_l.at[k], zl_s.at[k], zl_r.at[k])
        back = nn(gt_mat[...], zr_l[k].reshape(ZALL, COLS))
        lig_v[:, cols] = (acc[:, cols] + back).astype(BF)

    finish(0)
    finish(1)
    to_twin(ugr, ugr, 6).wait_recv()
    ug_v[...] += ugr[...]
    ug_copy = pltpu.make_async_copy(ug_v, ug_h, loc.at[11])
    ug_copy.start()
    finish(2)
    finish(3)
    lig_copy = pltpu.make_async_copy(lig_v, lig_h, loc.at[12])
    lig_copy.start()

    z_sent(zs_c, zc_s, zc_r)
    x_sent(xs_c, xc_s, xc_r)
    for k in range(1 + CHUNKS):
        z_sent(zs.at[k], z_s.at[k], z_r.at[k])
        x_sent(xs.at[k], x_s.at[k], x_r.at[k])
    for k in range(CHUNKS):
        z_sent(zs_l.at[k], zl_s.at[k], zl_r.at[k])
        x_sent(ls.at[k], xl_s.at[k], xl_r.at[k])
        to_twin(dgs.at[k], dgs.at[k], 2 + k).wait_send()
    to_twin(up_v.at[core], up_v.at[core], 0).wait_send()
    to_twin(dn_v.at[core], dn_v.at[core], 1).wait_send()
    to_twin(ugs, ugs, 6).wait_send()
    for n, buf in enumerate((ring, low, ring_u, low_u, cot_v, w_v)):
        for k in range(1, 4):
            t = lax.rem(y + k, 4)
            remote(buf.at[t], buf.at[t], y_s.at[n, t], y_r.at[n, t], narrow=t).wait_send()
    dg_copy.wait()
    ug_copy.wait()
    lig_copy.wait()


def on_device(
    tokens,
    cotangent,
    frozen_key_weight,
    adapter_down_maps,
    adapter_up_maps,
    previous_down_maps,
    previous_up_maps,
    down_fisher_diagonal,
    up_fisher_diagonal,
    token_adapter_index,
):
    vmem = pltpu.VMEM
    dma = pltpu.SemaphoreType.DMA
    scratch = [
        vmem((1, 512), jnp.int32), vmem((512, 1024), BF), vmem((4, 512, 256), BF), vmem((4, 1024, 256), BF),
        vmem((2, 512, 1024), BF), vmem((2, 512, 256), BF), vmem((512, 1024), BF), vmem((512, 256), BF),
        vmem((512, 1024), F32), vmem((512, 256), F32),
        vmem((512, 1024), BF), vmem((512, 1024), F32), vmem((512, 256), F32), vmem((512, 1024), F32),
        vmem((ZALL, 512), BF), vmem((512, ZALL), BF), vmem((ROWS, ZALL), BF), vmem((ZALL, ROWS), BF),
        vmem((5, 8, ZROWS, COLS), BF), vmem((5, 8, ZROWS, COLS), BF),
        vmem((8, 1, 128), F32), vmem((8, 1, 128), F32),
        vmem((5, 4, PACK, COLS), BF), vmem((5, 4, PACK, COLS), BF),
        vmem((4, 16, 384), BF), vmem((4, 16, 384), BF),
        vmem((4, 4, PACK, COLS), BF), vmem((4, 4, PACK, COLS), BF),
        vmem((4, 8, ZROWS, COLS), BF), vmem((4, 8, ZROWS, COLS), BF),
        vmem((4, PACK, 1024), BF), vmem((2, ROWS, 512), BF), vmem((2, ROWS, 512), BF),
        vmem((4, QUARTER, 128), F32), vmem((4, QUARTER, 128), F32), vmem((4, QUARTER, 128), BF),
        vmem((4, QUARTER, 128), F32), vmem((4, QUARTER, 128), F32), vmem((4, QUARTER, 128), BF),
        vmem((4, 512, COLS), F32), vmem((4, 512, COLS), F32), vmem((512, COLS), F32), vmem((512, COLS), F32),
        dma((13,)), dma((5, 8)), dma((5, 8)), dma((8,)), dma((8,)), dma((4, 8)), dma((4, 8)),
        dma((5, 4)), dma((5, 4)), dma((4,)), dma((4,)), dma((4, 4)), dma((4, 4)),
        dma((6, 4)), dma((6, 4)), dma((7,)), dma((7,)),
    ]
    flat = lambda a: a.reshape(512, -1)
    lig, dg, ug = pl.pallas_call(
        kernel,
        out_shape=(
            jax.ShapeDtypeStruct((512, 1024), BF),
            jax.ShapeDtypeStruct((512, 1024), F32),
            jax.ShapeDtypeStruct((512, 256), F32),
        ),
        in_specs=[pl.BlockSpec(memory_space=pl.ANY)] * 10,
        out_specs=[pl.BlockSpec(memory_space=pl.ANY)] * 3,
        scratch_shapes=scratch,
        compiler_params=pltpu.CompilerParams(
            collective_id=0, has_side_effects=True, vmem_limit_bytes=60 * 1024 * 1024
        ),
        cost_estimate=pl.CostEstimate(flops=12_000_000_000, bytes_accessed=12_000_000, transcendentals=0),
    )(
        token_adapter_index.reshape(1, 512),
        tokens,
        cotangent,
        frozen_key_weight,
        flat(adapter_down_maps),
        flat(adapter_up_maps),
        flat(previous_down_maps),
        flat(previous_up_maps),
        flat(down_fisher_diagonal),
        flat(up_fisher_diagonal),
    )
    return lig, dg.reshape(adapter_down_maps.shape), ug.reshape(adapter_up_maps.shape)


def solution(mesh):
    in_specs = (
        P("wide", "narrow"),
        P("wide", "narrow"),
        P(None, "narrow"),
        P("wide", None, "narrow"),
        P("wide", None, "narrow"),
        P("wide", None, "narrow"),
        P("wide", None, "narrow"),
        P("wide", None, "narrow"),
        P("wide", None, "narrow"),
        P("wide"),
    )
    out_specs = (P("wide", "narrow"), P("wide", None, "narrow"), P("wide", None, "narrow"))
    return jax.shard_map(
        on_device, mesh=mesh, in_specs=in_specs, out_specs=out_specs, check_vma=False
    )
```

```python
import jax
import jax.numpy as jnp
from jax import lax
from jax.experimental import pallas as pl
from jax.experimental.pallas import tpu as pltpu
from jax.sharding import PartitionSpec as P

MESH = pl.DeviceIdType.MESH
BF = jnp.bfloat16
F32 = jnp.float32

adapter_scale = 2.0
anchor_penalty_weight = 20.0

OFFSET = (1, 7, 2, 6, 3, 5, 4, 0)
MIRROR = (1, 0, 3, 2, 5, 4, 6, 7)
OWN = 7
ZROWS = 96
ZALL = 8 * ZROWS
SLOTS = 34
PACK = 8 * SLOTS
ROWS = 4 * PACK
HALF = 576
QUARTER = 144
COLS = 256
GRAD = ((0, 128), (128, 128))
ND = len(GRAD)
OUT = ((0, 256), (256, 256), (512, 256), (768, 256))
BACK = ((0, 256), (256, 256), (512, 256), (768, 256))


def iota(shape, dim):
    return lax.broadcasted_iota(jnp.int32, shape, dim)


def fiota(shape, dim):
    return iota(shape, dim).astype(F32)


def onehot(hit):
    return jnp.where(hit, 1.0, 0.0).astype(BF)


def nn(a, b):
    return jnp.dot(a, b, preferred_element_type=F32)


def nt(a, b):
    return lax.dot_general(a, b, (((1,), (1,)), ((), ())), preferred_element_type=F32)


def tn(a, b):
    return lax.dot_general(a, b, (((0,), (0,)), ((), ())), preferred_element_type=F32)


def remote(src, dst, send, recv, **where):
    return pltpu.make_async_remote_copy(
        src_ref=src, dst_ref=dst, send_sem=send, recv_sem=recv, device_id=where, device_id_type=MESH
    )


def offset_at(block):
    half = block >> 1
    return jnp.where(block == OWN, 0, jnp.where((block & 1) == 0, half + 1, 7 - half))


def kernel(
    idx_h, tok_h, cot_h, w_h, dn_h, up_h, pdn_h, pup_h, fd_h, fu_h,
    lig_h, dg_h, ug_h,
    idx_v, tok_v, cot_v, w_v, dn_v, up_v, pdn_v, pup_v, fd_v, fu_v,
    lig_v, dg_v, ug_v, acc,
    g_mat, gt_mat, p_mat, pt_mat,
    zs, zr, zs_c, zr_c, xs, xr, xs_c, xr_c, ls, lr, zs_l, zr_l,
    mask, spread, spread_u, part, ring, low, part_u, ring_u, low_u,
    dgs, dgr, held, xt, xt_c, mask_t,
    loc, z_s, z_r, zc_s, zc_r, zl_s, zl_r, x_s, x_r, xc_s, xc_r, xl_s, xl_r, y_s, y_r, c_s, c_r, u_s, u_r,
):
    wide = lax.axis_index("wide")
    y = lax.axis_index("narrow")
    z = wide // 8
    me = wide % 8
    x = me // 2
    core = me % 2
    twin = wide + 1 - 2 * core

    def z_dev(offset):
        return lax.rem(z + offset, 8) * 8 + me

    def x_at(k):
        return lax.rem(x + k, 4)

    def x_dev(t):
        return z * 8 + t * 2 + core

    bar = pltpu.get_barrier_semaphore()
    for k in range(1, 8):
        pl.semaphore_signal(bar, inc=1, device_id={"wide": z_dev(k)}, device_id_type=MESH)
    for k in range(1, 4):
        pl.semaphore_signal(bar, inc=1, device_id={"wide": x_dev(x_at(k))}, device_id_type=MESH)
        t = lax.rem(y + k, 4)
        pl.semaphore_signal(bar, inc=1, device_id={"narrow": t}, device_id_type=MESH)
        pl.semaphore_signal(bar, inc=1, device_id={"wide": twin, "narrow": t}, device_id_type=MESH)
    pl.semaphore_signal(bar, inc=1, device_id={"wide": twin}, device_id_type=MESH)

    local = [
        pltpu.make_async_copy(a, b, loc.at[i])
        for i, (a, b) in enumerate(
            [
                (idx_h, idx_v), (cot_h, cot_v.at[y]), (tok_h, tok_v), (up_h, up_v.at[core]), (dn_h, dn_v.at[core]),
                (w_h.at[pl.ds(pl.multiple_of(y * 1024, 1024), 1024)], w_v.at[y]),
                (pdn_h, pdn_v), (pup_h, pup_v), (fd_h, fd_v), (fu_h, fu_v),
            ]
        )
    ]
    for c in local:
        c.start()

    local[0].wait()
    hi = idx_v[...] >> 6
    code = ((idx_v[...] & 63) + 1).astype(F32)
    row = iota((8, 512), 0)
    hit = ((z + offset_at(row)) & 7) == hi
    rank = nn(onehot(hit), onehot(iota((512, 512), 0) < iota((512, 512), 1)))
    slot = jnp.sum(jnp.where(hit, rank + row.astype(F32) * ZROWS, 0.0), axis=0, keepdims=True)
    g_mat[...] = onehot(slot == fiota((ZALL, 512), 0))
    code16 = jnp.broadcast_to(code, (16, 512)).astype(BF)
    for b in range(8):
        sent = nt(code16, g_mat[b * ZROWS : (b + 1) * ZROWS, :])[:1]
        zs_c[b] = jnp.concatenate([sent, jnp.zeros((1, 128 - ZROWS), F32)], axis=1)
    local[1].wait()
    for k, (at, width) in enumerate(GRAD):
        packed = nn(g_mat[...], cot_v[y, :, at : at + width])
        zs[k][...] = packed.astype(BF).reshape(8, ZROWS, width)

    pl.semaphore_wait(bar, 17)

    def z_copy(src, dst, send, recv, b):
        return remote(src.at[b], dst.at[MIRROR[b]], send.at[b], recv.at[MIRROR[b]], wide=z_dev(OFFSET[b]))

    def z_start(src, dst, send, recv):
        for b in range(7):
            z_copy(src, dst, send, recv, b).start()
        dst[OWN] = src[OWN]

    def z_wait(dst, send, recv):
        for b in range(7):
            remote(dst.at[b], dst.at[b], send.at[b], recv.at[b], wide=z_dev(OFFSET[b])).wait_recv()

    def z_sent(src, send, recv):
        for b in range(7):
            remote(src.at[b], src.at[b], send.at[b], recv.at[b], wide=z_dev(OFFSET[b])).wait_send()

    def x_start(src, dst, send, recv):
        for k in range(1, 4):
            t = x_at(k)
            remote(src.at[t], dst.at[x], send.at[t], recv.at[x], wide=x_dev(t)).start()
        dst[x] = src[x]

    def x_wait(dst, send, recv):
        for k in range(1, 4):
            t = x_at(k)
            remote(dst.at[t], dst.at[t], send.at[t], recv.at[t], wide=x_dev(t)).wait_recv()

    def x_sent(src, send, recv):
        for k in range(1, 4):
            t = x_at(k)
            remote(src.at[t], src.at[t], send.at[t], recv.at[t], wide=x_dev(t)).wait_send()

    def to_twin(src, dst, n):
        return remote(src, dst, c_s.at[n], c_r.at[n], wide=twin)

    z_start(zs_c, zr_c, zc_s, zc_r)
    for k in range(ND):
        z_start(zs[k], zr[k], z_s.at[k], z_r.at[k])
    local[3].wait()
    local[4].wait()
    to_twin(up_v.at[core], up_v.at[core], 0).start()
    to_twin(dn_v.at[core], dn_v.at[core], 1).start()

    def y_share(buf, n):
        for k in range(1, 4):
            t = lax.rem(y + k, 4)
            remote(buf.at[y], buf.at[y], y_s.at[n, t], y_r.at[n, y], narrow=t).start()

    def y_wait(dst, n):
        for k in range(1, 4):
            t = lax.rem(y + k, 4)
            remote(dst.at[t], dst.at[t], y_s.at[n, t], y_r.at[n, t], narrow=t).wait_recv()

    y_share(cot_v, 4)
    local[2].wait()
    for k, (at, width) in enumerate(OUT, ND):
        packed = nn(g_mat[...], tok_v[:, at : at + width])
        zs[k][...] = packed.astype(BF).reshape(8, ZROWS, width)
        z_start(zs[k], zr[k], z_s.at[k], z_r.at[k])

    z_wait(zr_c, zc_s, zc_r)
    codes = zr_c[:, 0, :]
    upper = onehot(iota((128, 128), 0) < iota((128, 128), 1))
    place = jnp.zeros((8, 128), F32)
    for t in range(4):
        inside = (codes > 16.0 * t) & (codes < 16.0 * t + 17.0)
        spot = nn(onehot(inside), upper) + fiota((8, 128), 0) * SLOTS + float(t * PACK + 1)
        place = place + jnp.where(inside, spot, 0.0)
    place = jnp.concatenate([place[m : m + 1, :ZROWS] for m in range(8)], axis=1) - 1.0
    p_mat[...] = onehot(place == fiota((ROWS, ZALL), 0))
    line = jnp.concatenate([codes[m : m + 1, :ZROWS] for m in range(8)], axis=1)
    line = jnp.broadcast_to(line, (16, ZALL)).astype(BF)
    for t in range(4):
        sent = nt(line, p_mat[t * PACK : (t + 1) * PACK, :])
        xs_c[t] = jnp.concatenate([sent, jnp.zeros((16, 384 - PACK), F32)], axis=1).astype(BF)
    x_start(xs_c, xr_c, xc_s, xc_r)

    def repack(k):
        width = zr[k].shape[2]
        z_wait(zr[k], z_s.at[k], z_r.at[k])
        rows = nn(p_mat[...], zr[k][...].reshape(ZALL, width))
        xs[k][...] = rows.astype(BF).reshape(4, PACK, width)
        x_start(xs[k], xr[k], x_s.at[k], x_r.at[k])

    for k in range(ND):
        repack(k)

    codes32 = jnp.concatenate([jnp.broadcast_to(codes[m : m + 1], (4, 128)) for m in range(8)], axis=0)
    col = nt(onehot(iota((ZROWS, 128), 0) == iota((ZROWS, 128), 1)), codes32.astype(BF))
    lane = iota((ZROWS, 32), 1)
    first = (lane & 3).astype(F32) * 16.0
    inside = (col > first) & (col < first + 17.0)
    spot = nn(onehot(iota((ZROWS, ZROWS), 0) > iota((ZROWS, ZROWS), 1)), onehot(inside))
    spot = spot + ((lane & 3) * PACK + (lane >> 2) * SLOTS + 1).astype(F32)
    for m in range(8):
        at = jnp.sum(jnp.where(inside & ((lane >> 2) == m), spot, 0.0), axis=1, keepdims=True) - 1.0
        pt_mat[m * ZROWS : (m + 1) * ZROWS, :] = onehot(at == fiota((ZROWS, ROWS), 1))

    def named(codes, t, lanes, base):
        seen = nt(onehot(iota((PACK, 384), 0) == iota((PACK, 384), 1)), codes[t])[:, :1]
        return onehot(seen == (iota((PACK, lanes), 1) // 64 + base).astype(F32))

    x_wait(xr_c, xc_s, xc_r)
    for t in range(4):
        mask[t] = named(xr_c, t, 1024, 1 + 16 * x)

    def fold(every, t):
        kept = every * mask[t].astype(F32)
        total = kept[:, :128]
        for j in range(1, 8):
            total = total + kept[:, j * 128 : (j + 1) * 128]
        return total + pltpu.roll(total, 64, 1)

    left = iota((HALF, 128), 1) < 64

    def arrive(k):
        x_wait(xr[k], x_s.at[k], x_r.at[k])

    def rank_rows(maps, chunks, ks):
        sums = []
        for t in range(4):
            every = None
            for k in ks:
                at, width = chunks[k] if chunks is GRAD else chunks[k - ND]
                one = nt(xr[k][t], maps[:, :, at : at + width].reshape(1024, width))
                every = one if every is None else every + one
            sums.append(fold(every, t))
        return jnp.concatenate(sums, axis=0)

    def sum_start(rows, source, dst, n):
        lower = jnp.concatenate([rows[HALF:], jnp.zeros((2 * HALF - ROWS, 128), F32)], axis=0)
        source[...] = jnp.where(left, rows[:HALF], lower).reshape(4, QUARTER, 128)
        for k in range(1, 4):
            t = lax.rem(y + k, 4)
            remote(source.at[t], dst.at[y], y_s.at[n, t], y_r.at[n, y], narrow=t).start()
        dst[y] = source[y]

    def sum_share(src, dst, n):
        y_wait(src, n)
        dst[y] = ((src[0] + src[1]) + (src[2] + src[3])).astype(BF)
        y_share(dst, n + 1)

    def rank_pairs(buf):
        value = buf[...].reshape(HALF, 128).astype(F32)
        other = pltpu.roll(value, 64, 1)
        high = jnp.where(left, value, other).astype(BF)
        rest = jnp.where(left, other, value).astype(BF)
        return jnp.concatenate([high, rest[: ROWS - HALF]], axis=0)

    def spread_of(buf, out):
        both = rank_pairs(buf)
        for t in range(4):
            one = jnp.concatenate([both[t * PACK : (t + 1) * PACK]] * 4, axis=1)
            for c in range(2):
                out[c, t * PACK : (t + 1) * PACK, :] = one * mask[t, :, c * 512 : (c + 1) * 512]

    to_twin(up_v.at[1 - core], up_v.at[1 - core], 0).wait_recv()
    repack(ND)
    for k in range(ND):
        arrive(k)
    sum_start(rank_rows(up_v, GRAD, range(ND)), part, ring, 0)
    for k in range(ND):
        to_twin(xr[k], xt[k], 2 + k).start()
    to_twin(xr_c, xt_c, 2 + ND).start()
    sum_share(ring, low, 0)
    repack(ND + 1)
    for k in range(1, 4):
        t = lax.rem(y + k, 4)
        remote(
            w_h.at[pl.ds(pl.multiple_of(t * 1024, 1024), 1024)],
            w_v.at[y], y_s.at[5, t], y_r.at[5, y], narrow=t,
        ).start()
    to_twin(dn_v.at[1 - core], dn_v.at[1 - core], 1).wait_recv()
    y_wait(low, 1)
    spread_of(low, spread)

    def lora(k):
        at, width = BACK[k]
        rows = nn(spread[0], dn_v[0, :, at : at + width])
        rows = rows + nn(spread[1], dn_v[1, :, at : at + width])
        ls[k][...] = (adapter_scale * rows).astype(BF).reshape(4, PACK, width)
        x_start(ls[k], lr[k], xl_s.at[k], xl_r.at[k])

    def unpack(k):
        width = BACK[k][1]
        x_wait(lr[k], xl_s.at[k], xl_r.at[k])
        rows = nn(pt_mat[...], lr[k][...].reshape(ROWS, width)).astype(BF)
        zs_l[k][...] = rows.reshape(8, ZROWS, width)
        z_start(zs_l[k], zr_l[k], zl_s.at[k], zl_r.at[k])

    def penalties():
        for i in range(6, 10):
            local[i].wait()

        def down(i, carry):
            at = pl.ds(pl.multiple_of(i * 64, 64), 64)
            delta = dn_v[core, at, :].astype(F32) - pdn_v[at, :].astype(F32)
            dg_v[at, :] = anchor_penalty_weight * fd_v[at, :] * delta
            return carry

        lax.fori_loop(0, 8, down, 0)
        delta = up_v[core].astype(F32) - pup_v[...].astype(F32)
        ug_v[...] = anchor_penalty_weight * fu_v[...] * delta

    def return_map():
        hi16 = jnp.broadcast_to(hi, (16, 512)).astype(F32).astype(BF)
        hi_col = nt(onehot(iota((512, 512), 0) == iota((512, 512), 1)), hi16)[:, :1]
        lane = iota((512, 128), 1)
        hit = (((z + offset_at(lane)) & 7).astype(F32) == hi_col) & (lane < 8)
        rank = nn(onehot(iota((512, 512), 0) > iota((512, 512), 1)), onehot(hit))
        slot_col = jnp.where(hit, rank + lane.astype(F32) * ZROWS, 0.0)
        slot_col = jnp.sum(slot_col, axis=1, keepdims=True)
        gt_mat[...] = onehot(slot_col == fiota((512, ZALL), 1))

    def gradient(k):
        at, width = OUT[k]
        rows = xr[ND + k][...].reshape(ROWS, width)
        dgs[k][...] = adapter_scale * tn(spread[1 - core], rows)
        to_twin(dgs[k], dgr[k], 3 + ND + k).start()
        dg_v[:, at : at + width] += adapter_scale * tn(spread[core], rows)

    def frozen():
        y_wait(cot_v, 4)
        local[5].wait()
        y_wait(w_v, 5)

        def one(i, carry):
            at = pl.ds(pl.multiple_of(i * 128, 128), 128)
            total = nt(cot_v[0, at, :], w_v[0])
            for j in range(1, 4):
                total = total + nt(cot_v[j, at, :], w_v[j])
            acc[at, :] = total
            return carry

        lax.fori_loop(0, 4, one, 0)

    lig_copies = []

    def finish(k):
        at, width = BACK[k]
        z_wait(zr_l[k], zl_s.at[k], zl_r.at[k])
        back = nn(gt_mat[...], zr_l[k][...].reshape(ZALL, width))
        lig_v[k][...] = (acc[:, at : at + width] + back).astype(BF)
        lig_copies.append(
            pltpu.make_async_copy(lig_v[k], lig_h.at[:, pl.ds(at, width)], loc.at[12 + k])
        )
        lig_copies[-1].start()

    lora(0)
    lora(1)
    repack(ND + 2)
    lora(2)
    repack(ND + 3)
    lora(3)
    penalties()
    unpack(0)
    return_map()
    to_twin(xt_c, xt_c, 2 + ND).wait_recv()
    for t in range(4):
        mask_t[t] = named(xt_c, t, 512, 1 + 16 * x + 8 * core)
    arrive(ND + 0)
    gradient(0)
    arrive(ND + 1)
    gradient(1)
    unpack(1)
    frozen()
    arrive(ND + 2)
    gradient(2)
    held[...] = rank_rows(dn_v, OUT, (ND, ND + 1, ND + 2))
    unpack(2)
    arrive(ND + 3)
    sum_start(held[...] + rank_rows(dn_v, OUT, (ND + 3,)), part_u, ring_u, 2)
    unpack(3)
    gradient(3)
    y_wait(ring_u, 2)
    low_u[core, y] = ((ring_u[0] + ring_u[1]) + (ring_u[2] + ring_u[3])).astype(BF)
    for k in range(1, 4):
        t = lax.rem(y + k, 4)
        remote(low_u.at[core, y], low_u.at[core, y], y_s.at[3, t], y_r.at[3, y], narrow=t).start()
    for k in range(4):
        t = lax.rem(y + k, 4)
        remote(
            low_u.at[core, y], low_u.at[core, y], u_s.at[t], u_r.at[y], wide=twin, narrow=t
        ).start()
    finish(0)
    for k, (at, width) in enumerate(OUT):
        to_twin(dgr[k], dgr[k], 3 + ND + k).wait_recv()
        dg_v[:, at : at + width] += dgr[k][...]
    dg_copy = pltpu.make_async_copy(dg_v, dg_h, loc.at[10])
    dg_copy.start()
    finish(1)
    for k in range(ND):
        to_twin(xt[k], xt[k], 2 + k).wait_recv()
    for k in range(1, 4):
        t = lax.rem(y + k, 4)
        remote(low_u.at[core, t], low_u.at[core, t], y_s.at[3, t], y_r.at[3, t], narrow=t).wait_recv()
    for k in range(4):
        t = lax.rem(y + k, 4)
        remote(
            low_u.at[1 - core, t], low_u.at[1 - core, t], u_s.at[t], u_r.at[t], wide=twin, narrow=t
        ).wait_recv()
    mine, theirs = rank_pairs(low_u.at[core]), rank_pairs(low_u.at[1 - core])
    for t in range(4):
        part_of = slice(t * PACK, (t + 1) * PACK)
        wide_mask = jnp.where(core == 0, mask[t, :, :512], mask[t, :, 512:])
        spread_u[0, part_of, :] = jnp.concatenate([mine[part_of]] * 4, axis=1) * wide_mask
        spread_u[1, part_of, :] = jnp.concatenate([theirs[part_of]] * 4, axis=1) * mask_t[t]
    for k, (at, width) in enumerate(GRAD):
        both = tn(spread_u[0], xr[k][...].reshape(ROWS, width))
        both = both + tn(spread_u[1], xt[k][...].reshape(ROWS, width))
        ug_v[:, at : at + width] += adapter_scale * both
    ug_copy = pltpu.make_async_copy(ug_v, ug_h, loc.at[11])
    ug_copy.start()
    for k in range(2, len(BACK)):
        finish(k)

    z_sent(zs_c, zc_s, zc_r)
    x_sent(xs_c, xc_s, xc_r)
    for k in range(len(OUT) + ND):
        z_sent(zs[k], z_s.at[k], z_r.at[k])
        x_sent(xs[k], x_s.at[k], x_r.at[k])
    for k in range(len(OUT)):
        to_twin(dgs[k], dgs[k], 3 + ND + k).wait_send()
    for k in range(ND):
        to_twin(xr[k], xr[k], 2 + k).wait_send()
    to_twin(xr_c, xr_c, 2 + ND).wait_send()
    for k in range(len(BACK)):
        z_sent(zs_l[k], zl_s.at[k], zl_r.at[k])
        x_sent(ls[k], xl_s.at[k], xl_r.at[k])
    to_twin(up_v.at[core], up_v.at[core], 0).wait_send()
    to_twin(dn_v.at[core], dn_v.at[core], 1).wait_send()
    for k in range(4):
        t = lax.rem(y + k, 4)
        remote(low_u.at[0, t], low_u.at[0, t], u_s.at[t], u_r.at[t], wide=twin, narrow=t).wait_send()
    for n, buf in enumerate((ring, low, ring_u, low_u.at[0], cot_v, w_v)):
        for k in range(1, 4):
            t = lax.rem(y + k, 4)
            remote(buf.at[t], buf.at[t], y_s.at[n, t], y_r.at[n, t], narrow=t).wait_send()
    dg_copy.wait()
    ug_copy.wait()
    for c in lig_copies:
        c.wait()


def deliver(lig, dg, ug, lig_out, dg_out, ug_out, lig_v, dg_v, ug_v, into, back):
    inward, outward = [], []
    for src, held, dst, parts in ((dg, dg_v, dg_out, 4), (lig, lig_v, lig_out, 2), (ug, ug_v, ug_out, 1)):
        for i in range(parts):
            at = pl.ds(i * (512 // parts), 512 // parts)
            n = len(inward)
            inward.append(pltpu.make_async_copy(src.at[at], held.at[at], into.at[n]))
            outward.append(pltpu.make_async_copy(held.at[at], dst.at[at], back.at[n]))
    for c in inward:
        c.start()
    for c, d in zip(inward, outward):
        c.wait()
        d.start()
    for d in outward:
        d.wait()


def on_device(
    tokens,
    cotangent,
    frozen_key_weight,
    adapter_down_maps,
    adapter_up_maps,
    previous_down_maps,
    previous_up_maps,
    down_fisher_diagonal,
    up_fisher_diagonal,
    token_adapter_index,
):
    vmem = pltpu.VMEM
    dma = pltpu.SemaphoreType.DMA
    no, nb = len(OUT) + ND, len(BACK)
    RANKED = GRAD + OUT
    each = lambda chunks, dims, kind: tuple(vmem((*dims, width), kind) for _, width in chunks)
    scratch = [
        vmem((1, 512), jnp.int32), vmem((512, 1024), BF), vmem((4, 512, 256), BF), vmem((4, 1024, 256), BF),
        vmem((2, 512, 1024), BF), vmem((2, 512, 256), BF), vmem((512, 1024), BF), vmem((512, 256), BF),
        vmem((512, 1024), F32), vmem((512, 256), F32),
        each(BACK, (512,), BF), vmem((512, 1024), F32), vmem((512, 256), F32), vmem((512, 1024), F32),
        vmem((ZALL, 512), BF), vmem((512, ZALL), BF), vmem((ROWS, ZALL), BF), vmem((ZALL, ROWS), BF),
        each(RANKED, (8, ZROWS), BF), each(RANKED, (8, ZROWS), BF),
        vmem((8, 1, 128), F32), vmem((8, 1, 128), F32),
        each(RANKED, (4, PACK), BF), each(RANKED, (4, PACK), BF),
        vmem((4, 16, 384), BF), vmem((4, 16, 384), BF),
        each(BACK, (4, PACK), BF), each(BACK, (4, PACK), BF),
        each(BACK, (8, ZROWS), BF), each(BACK, (8, ZROWS), BF),
        vmem((4, PACK, 1024), BF), vmem((2, ROWS, 512), BF), vmem((2, ROWS, 512), BF),
        vmem((4, QUARTER, 128), F32), vmem((4, QUARTER, 128), F32), vmem((4, QUARTER, 128), BF),
        vmem((4, QUARTER, 128), F32), vmem((4, QUARTER, 128), F32), vmem((2, 4, QUARTER, 128), BF),
        each(OUT, (512,), F32), each(OUT, (512,), F32),
        vmem((ROWS, 128), F32), each(GRAD, (4, PACK), BF), vmem((4, 16, 384), BF), vmem((4, PACK, 512), BF),
        dma((12 + nb,)), dma((no, 8)), dma((no, 8)), dma((8,)), dma((8,)), dma((nb, 8)), dma((nb, 8)),
        dma((no, 4)), dma((no, 4)), dma((4,)), dma((4,)), dma((nb, 4)), dma((nb, 4)),
        dma((6, 4)), dma((6, 4)), dma((3 + no,)), dma((3 + no,)), dma((4,)), dma((4,)),
    ]
    flat = lambda a: a.reshape(512, -1)
    lig, dg, ug = pl.pallas_call(
        kernel,
        out_shape=(
            jax.ShapeDtypeStruct((512, 1024), BF),
            jax.ShapeDtypeStruct((512, 1024), F32),
            jax.ShapeDtypeStruct((512, 256), F32),
        ),
        in_specs=[pl.BlockSpec(memory_space=pl.ANY)] * 10,
        out_specs=[pl.BlockSpec(memory_space=pl.ANY)] * 3,
        scratch_shapes=scratch,
        compiler_params=pltpu.CompilerParams(
            collective_id=0, has_side_effects=True, vmem_limit_bytes=60 * 1024 * 1024
        ),
        cost_estimate=pl.CostEstimate(flops=12_000_000_000, bytes_accessed=12_000_000, transcendentals=0),
    )(
        token_adapter_index.reshape(1, 512),
        tokens,
        cotangent,
        frozen_key_weight,
        flat(adapter_down_maps),
        flat(adapter_up_maps),
        flat(previous_down_maps),
        flat(previous_up_maps),
        flat(down_fisher_diagonal),
        flat(up_fisher_diagonal),
    )
    whole = pl.BlockSpec(memory_space=pl.ANY)
    lig, dg, ug = pl.pallas_call(
        deliver,
        out_shape=tuple(jax.ShapeDtypeStruct(a.shape, a.dtype) for a in (lig, dg, ug)),
        in_specs=[whole] * 3,
        out_specs=[whole] * 3,
        scratch_shapes=[vmem(a.shape, a.dtype) for a in (lig, dg, ug)] + [dma((7,)), dma((7,))],
        compiler_params=pltpu.CompilerParams(vmem_limit_bytes=60 * 1024 * 1024),
        cost_estimate=pl.CostEstimate(flops=0, bytes_accessed=7_340_032, transcendentals=0),
    )(lig, dg, ug)
    return lig, dg.reshape(adapter_down_maps.shape), ug.reshape(adapter_up_maps.shape)


def solution(mesh):
    in_specs = (
        P("wide", "narrow"),
        P("wide", "narrow"),
        P(None, "narrow"),
        P("wide", None, "narrow"),
        P("wide", None, "narrow"),
        P("wide", None, "narrow"),
        P("wide", None, "narrow"),
        P("wide", None, "narrow"),
        P("wide", None, "narrow"),
        P("wide"),
    )
    out_specs = (P("wide", "narrow"), P("wide", None, "narrow"), P("wide", None, "narrow"))
    return jax.shard_map(
        on_device, mesh=mesh, in_specs=in_specs, out_specs=out_specs, check_vma=False
    )
```

```python
import jax
import jax.numpy as jnp
from jax import lax
from jax.experimental import pallas as pl
from jax.experimental.pallas import tpu as pltpu
from jax.sharding import PartitionSpec as P

MESH = pl.DeviceIdType.MESH
BF = jnp.bfloat16
F32 = jnp.float32

adapter_scale = 2.0
anchor_penalty_weight = 20.0

OFFSET = (1, 7, 2, 6, 3, 5, 4, 0)
MIRROR = (1, 0, 3, 2, 5, 4, 6, 7)
OWN = 7
ZROWS = 96
ZALL = 8 * ZROWS
SLOTS = 34
PACK = 8 * SLOTS
ROWS = 4 * PACK
HALF = 576
QUARTER = 144
COLS = 256
GRAD = ((0, 128), (128, 128))
ND = len(GRAD)
OUT = ((0, 256), (256, 256), (512, 256), (768, 256))
BACK = ((0, 256), (256, 256), (512, 256), (768, 256))


def iota(shape, dim):
    return lax.broadcasted_iota(jnp.int32, shape, dim)


def fiota(shape, dim):
    return iota(shape, dim).astype(F32)


def onehot(hit):
    return jnp.where(hit, 1.0, 0.0).astype(BF)


def nn(a, b):
    return jnp.dot(a, b, preferred_element_type=F32)


def nt(a, b):
    return lax.dot_general(a, b, (((1,), (1,)), ((), ())), preferred_element_type=F32)


def tn(a, b):
    return lax.dot_general(a, b, (((0,), (0,)), ((), ())), preferred_element_type=F32)


def remote(src, dst, send, recv, **where):
    return pltpu.make_async_remote_copy(
        src_ref=src, dst_ref=dst, send_sem=send, recv_sem=recv, device_id=where, device_id_type=MESH
    )


def offset_at(block):
    half = block >> 1
    return jnp.where(block == OWN, 0, jnp.where((block & 1) == 0, half + 1, 7 - half))


def kernel(
    idx_h, tok_h, cot_h, w_h, dn_h, up_h, pdn_h, pup_h, fd_h, fu_h,
    lig_0, lig_1, lig_2, lig_3, dg_v, ug_v,
    idx_v, tok_v, cot_v, w_v, dn_v, up_v, pdn_v, pup_v, fd_v, fu_v,
    acc,
    g_mat, gt_mat, p_mat, pt_mat,
    zs, zr, zs_c, zr_c, xs, xr, xs_c, xr_c, ls, lr, zs_l, zr_l,
    mask, spread, spread_u, part, ring, low, part_u, ring_u, low_u,
    dgs, dgr, held, xt, xt_c, mask_t,
    loc, z_s, z_r, zc_s, zc_r, zl_s, zl_r, x_s, x_r, xc_s, xc_r, xl_s, xl_r, y_s, y_r, c_s, c_r, u_s, u_r,
):
    lig_v = (lig_0, lig_1, lig_2, lig_3)
    wide = lax.axis_index("wide")
    y = lax.axis_index("narrow")
    z = wide // 8
    me = wide % 8
    x = me // 2
    core = me % 2
    twin = wide + 1 - 2 * core

    def z_dev(offset):
        return lax.rem(z + offset, 8) * 8 + me

    def x_at(k):
        return lax.rem(x + k, 4)

    def x_dev(t):
        return z * 8 + t * 2 + core

    bar = pltpu.get_barrier_semaphore()
    for k in range(1, 8):
        pl.semaphore_signal(bar, inc=1, device_id={"wide": z_dev(k)}, device_id_type=MESH)
    for k in range(1, 4):
        pl.semaphore_signal(bar, inc=1, device_id={"wide": x_dev(x_at(k))}, device_id_type=MESH)
        t = lax.rem(y + k, 4)
        pl.semaphore_signal(bar, inc=1, device_id={"narrow": t}, device_id_type=MESH)
        pl.semaphore_signal(bar, inc=1, device_id={"wide": twin, "narrow": t}, device_id_type=MESH)
    pl.semaphore_signal(bar, inc=1, device_id={"wide": twin}, device_id_type=MESH)

    local = [
        pltpu.make_async_copy(a, b, loc.at[i])
        for i, (a, b) in enumerate(
            [
                (idx_h, idx_v), (cot_h, cot_v.at[y]), (tok_h, tok_v), (up_h, up_v.at[core]), (dn_h, dn_v.at[core]),
                (w_h.at[pl.ds(pl.multiple_of(y * 1024, 1024), 1024)], w_v.at[y]),
                (pdn_h, pdn_v), (pup_h, pup_v), (fd_h, fd_v), (fu_h, fu_v),
            ]
        )
    ]
    for c in local:
        c.start()

    local[0].wait()
    hi = idx_v[...] >> 6
    code = ((idx_v[...] & 63) + 1).astype(F32)
    row = iota((8, 512), 0)
    hit = ((z + offset_at(row)) & 7) == hi
    rank = nn(onehot(hit), onehot(iota((512, 512), 0) < iota((512, 512), 1)))
    slot = jnp.sum(jnp.where(hit, rank + row.astype(F32) * ZROWS, 0.0), axis=0, keepdims=True)
    g_mat[...] = onehot(slot == fiota((ZALL, 512), 0))
    code16 = jnp.broadcast_to(code, (16, 512)).astype(BF)
    for b in range(8):
        sent = nt(code16, g_mat[b * ZROWS : (b + 1) * ZROWS, :])[:1]
        zs_c[b] = jnp.concatenate([sent, jnp.zeros((1, 128 - ZROWS), F32)], axis=1)
    local[1].wait()
    for k, (at, width) in enumerate(GRAD):
        packed = nn(g_mat[...], cot_v[y, :, at : at + width])
        zs[k][...] = packed.astype(BF).reshape(8, ZROWS, width)

    pl.semaphore_wait(bar, 17)

    def z_copy(src, dst, send, recv, b):
        return remote(src.at[b], dst.at[MIRROR[b]], send.at[b], recv.at[MIRROR[b]], wide=z_dev(OFFSET[b]))

    def z_start(src, dst, send, recv):
        for b in range(7):
            z_copy(src, dst, send, recv, b).start()
        dst[OWN] = src[OWN]

    def z_wait(dst, send, recv):
        for b in range(7):
            remote(dst.at[b], dst.at[b], send.at[b], recv.at[b], wide=z_dev(OFFSET[b])).wait_recv()

    def z_sent(src, send, recv):
        for b in range(7):
            remote(src.at[b], src.at[b], send.at[b], recv.at[b], wide=z_dev(OFFSET[b])).wait_send()

    def x_start(src, dst, send, recv):
        for k in range(1, 4):
            t = x_at(k)
            remote(src.at[t], dst.at[x], send.at[t], recv.at[x], wide=x_dev(t)).start()
        dst[x] = src[x]

    def x_wait(dst, send, recv):
        for k in range(1, 4):
            t = x_at(k)
            remote(dst.at[t], dst.at[t], send.at[t], recv.at[t], wide=x_dev(t)).wait_recv()

    def x_sent(src, send, recv):
        for k in range(1, 4):
            t = x_at(k)
            remote(src.at[t], src.at[t], send.at[t], recv.at[t], wide=x_dev(t)).wait_send()

    def to_twin(src, dst, n):
        return remote(src, dst, c_s.at[n], c_r.at[n], wide=twin)

    z_start(zs_c, zr_c, zc_s, zc_r)
    for k in range(ND):
        z_start(zs[k], zr[k], z_s.at[k], z_r.at[k])
    local[3].wait()
    local[4].wait()
    to_twin(up_v.at[core], up_v.at[core], 0).start()
    to_twin(dn_v.at[core], dn_v.at[core], 1).start()

    def y_share(buf, n):
        for k in range(1, 4):
            t = lax.rem(y + k, 4)
            remote(buf.at[y], buf.at[y], y_s.at[n, t], y_r.at[n, y], narrow=t).start()

    def y_wait(dst, n):
        for k in range(1, 4):
            t = lax.rem(y + k, 4)
            remote(dst.at[t], dst.at[t], y_s.at[n, t], y_r.at[n, t], narrow=t).wait_recv()

    y_share(cot_v, 4)
    local[2].wait()
    for k, (at, width) in enumerate(OUT, ND):
        packed = nn(g_mat[...], tok_v[:, at : at + width])
        zs[k][...] = packed.astype(BF).reshape(8, ZROWS, width)
        z_start(zs[k], zr[k], z_s.at[k], z_r.at[k])

    z_wait(zr_c, zc_s, zc_r)
    codes = zr_c[:, 0, :]
    upper = onehot(iota((128, 128), 0) < iota((128, 128), 1))
    place = jnp.zeros((8, 128), F32)
    for t in range(4):
        inside = (codes > 16.0 * t) & (codes < 16.0 * t + 17.0)
        spot = nn(onehot(inside), upper) + fiota((8, 128), 0) * SLOTS + float(t * PACK + 1)
        place = place + jnp.where(inside, spot, 0.0)
    place = jnp.concatenate([place[m : m + 1, :ZROWS] for m in range(8)], axis=1) - 1.0
    p_mat[...] = onehot(place == fiota((ROWS, ZALL), 0))
    line = jnp.concatenate([codes[m : m + 1, :ZROWS] for m in range(8)], axis=1)
    line = jnp.broadcast_to(line, (16, ZALL)).astype(BF)
    for t in range(4):
        sent = nt(line, p_mat[t * PACK : (t + 1) * PACK, :])
        xs_c[t] = jnp.concatenate([sent, jnp.zeros((16, 384 - PACK), F32)], axis=1).astype(BF)
    x_start(xs_c, xr_c, xc_s, xc_r)

    def repack(k):
        width = zr[k].shape[2]
        z_wait(zr[k], z_s.at[k], z_r.at[k])
        rows = nn(p_mat[...], zr[k][...].reshape(ZALL, width))
        xs[k][...] = rows.astype(BF).reshape(4, PACK, width)
        x_start(xs[k], xr[k], x_s.at[k], x_r.at[k])

    for k in range(ND):
        repack(k)

    codes32 = jnp.concatenate([jnp.broadcast_to(codes[m : m + 1], (4, 128)) for m in range(8)], axis=0)
    col = nt(onehot(iota((ZROWS, 128), 0) == iota((ZROWS, 128), 1)), codes32.astype(BF))
    lane = iota((ZROWS, 32), 1)
    first = (lane & 3).astype(F32) * 16.0
    inside = (col > first) & (col < first + 17.0)
    spot = nn(onehot(iota((ZROWS, ZROWS), 0) > iota((ZROWS, ZROWS), 1)), onehot(inside))
    spot = spot + ((lane & 3) * PACK + (lane >> 2) * SLOTS + 1).astype(F32)
    for m in range(8):
        at = jnp.sum(jnp.where(inside & ((lane >> 2) == m), spot, 0.0), axis=1, keepdims=True) - 1.0
        pt_mat[m * ZROWS : (m + 1) * ZROWS, :] = onehot(at == fiota((ZROWS, ROWS), 1))

    def named(codes, t, lanes, base):
        seen = nt(onehot(iota((PACK, 384), 0) == iota((PACK, 384), 1)), codes[t])[:, :1]
        return onehot(seen == (iota((PACK, lanes), 1) // 64 + base).astype(F32))

    x_wait(xr_c, xc_s, xc_r)
    for t in range(4):
        mask[t] = named(xr_c, t, 1024, 1 + 16 * x)

    def fold(every, t):
        kept = every * mask[t].astype(F32)
        total = kept[:, :128]
        for j in range(1, 8):
            total = total + kept[:, j * 128 : (j + 1) * 128]
        return total + pltpu.roll(total, 64, 1)

    left = iota((HALF, 128), 1) < 64

    def arrive(k):
        x_wait(xr[k], x_s.at[k], x_r.at[k])

    def rank_rows(maps, chunks, ks):
        sums = []
        for t in range(4):
            every = None
            for k in ks:
                at, width = chunks[k] if chunks is GRAD else chunks[k - ND]
                one = nt(xr[k][t], maps[:, :, at : at + width].reshape(1024, width))
                every = one if every is None else every + one
            sums.append(fold(every, t))
        return jnp.concatenate(sums, axis=0)

    def sum_start(rows, source, dst, n):
        lower = jnp.concatenate([rows[HALF:], jnp.zeros((2 * HALF - ROWS, 128), F32)], axis=0)
        source[...] = jnp.where(left, rows[:HALF], lower).reshape(4, QUARTER, 128)
        for k in range(1, 4):
            t = lax.rem(y + k, 4)
            remote(source.at[t], dst.at[y], y_s.at[n, t], y_r.at[n, y], narrow=t).start()
        dst[y] = source[y]

    def sum_share(src, dst, n):
        y_wait(src, n)
        dst[y] = ((src[0] + src[1]) + (src[2] + src[3])).astype(BF)
        y_share(dst, n + 1)

    def rank_pairs(buf):
        value = buf[...].reshape(HALF, 128).astype(F32)
        other = pltpu.roll(value, 64, 1)
        high = jnp.where(left, value, other).astype(BF)
        rest = jnp.where(left, other, value).astype(BF)
        return jnp.concatenate([high, rest[: ROWS - HALF]], axis=0)

    def spread_of(buf, out):
        both = rank_pairs(buf)
        for t in range(4):
            one = jnp.concatenate([both[t * PACK : (t + 1) * PACK]] * 4, axis=1)
            for c in range(2):
                out[c, t * PACK : (t + 1) * PACK, :] = one * mask[t, :, c * 512 : (c + 1) * 512]

    to_twin(up_v.at[1 - core], up_v.at[1 - core], 0).wait_recv()
    repack(ND)
    for k in range(ND):
        arrive(k)
    sum_start(rank_rows(up_v, GRAD, range(ND)), part, ring, 0)
    for k in range(ND):
        to_twin(xr[k], xt[k], 2 + k).start()
    to_twin(xr_c, xt_c, 2 + ND).start()
    sum_share(ring, low, 0)
    repack(ND + 1)
    for k in range(1, 4):
        t = lax.rem(y + k, 4)
        remote(
            w_h.at[pl.ds(pl.multiple_of(t * 1024, 1024), 1024)],
            w_v.at[y], y_s.at[5, t], y_r.at[5, y], narrow=t,
        ).start()
    def penalties():
        for i in range(6, 10):
            local[i].wait()

        def down(i, carry):
            at = pl.ds(pl.multiple_of(i * 64, 64), 64)
            delta = dn_v[core, at, :].astype(F32) - pdn_v[at, :].astype(F32)
            dg_v[at, :] = anchor_penalty_weight * fd_v[at, :] * delta
            return carry

        lax.fori_loop(0, 8, down, 0)
        delta = up_v[core].astype(F32) - pup_v[...].astype(F32)
        ug_v[...] = anchor_penalty_weight * fu_v[...] * delta

    def return_map():
        hi16 = jnp.broadcast_to(hi, (16, 512)).astype(F32).astype(BF)
        hi_col = nt(onehot(iota((512, 512), 0) == iota((512, 512), 1)), hi16)[:, :1]
        lane = iota((512, 128), 1)
        hit = (((z + offset_at(lane)) & 7).astype(F32) == hi_col) & (lane < 8)
        rank = nn(onehot(iota((512, 512), 0) > iota((512, 512), 1)), onehot(hit))
        slot_col = jnp.where(hit, rank + lane.astype(F32) * ZROWS, 0.0)
        slot_col = jnp.sum(slot_col, axis=1, keepdims=True)
        gt_mat[...] = onehot(slot_col == fiota((512, ZALL), 1))

    penalties()
    return_map()
    to_twin(xt_c, xt_c, 2 + ND).wait_recv()
    for t in range(4):
        mask_t[t] = named(xt_c, t, 512, 1 + 16 * x + 8 * core)
    to_twin(dn_v.at[1 - core], dn_v.at[1 - core], 1).wait_recv()
    y_wait(low, 1)
    spread_of(low, spread)

    def lora(k):
        at, width = BACK[k]
        rows = nn(spread[0], dn_v[0, :, at : at + width])
        rows = rows + nn(spread[1], dn_v[1, :, at : at + width])
        ls[k][...] = (adapter_scale * rows).astype(BF).reshape(4, PACK, width)
        x_start(ls[k], lr[k], xl_s.at[k], xl_r.at[k])

    def unpack(k):
        width = BACK[k][1]
        x_wait(lr[k], xl_s.at[k], xl_r.at[k])
        rows = nn(pt_mat[...], lr[k][...].reshape(ROWS, width)).astype(BF)
        zs_l[k][...] = rows.reshape(8, ZROWS, width)
        z_start(zs_l[k], zr_l[k], zl_s.at[k], zl_r.at[k])

    def gradient(k):
        at, width = OUT[k]
        rows = xr[ND + k][...].reshape(ROWS, width)
        dgs[k][...] = adapter_scale * tn(spread[1 - core], rows)
        to_twin(dgs[k], dgr[k], 3 + ND + k).start()
        dg_v[:, at : at + width] += adapter_scale * tn(spread[core], rows)

    def frozen():
        y_wait(cot_v, 4)
        local[5].wait()
        y_wait(w_v, 5)

        def one(i, carry):
            at = pl.ds(pl.multiple_of(i * 128, 128), 128)
            total = nt(cot_v[0, at, :], w_v[0])
            for j in range(1, 4):
                total = total + nt(cot_v[j, at, :], w_v[j])
            acc[at, :] = total
            return carry

        lax.fori_loop(0, 4, one, 0)


    def finish(k):
        at, width = BACK[k]
        z_wait(zr_l[k], zl_s.at[k], zl_r.at[k])
        back = nn(gt_mat[...], zr_l[k][...].reshape(ZALL, width))
        lig_v[k][...] = (acc[:, at : at + width] + back).astype(BF)

    lora(0)
    lora(1)
    repack(ND + 2)
    lora(2)
    arrive(ND + 0)
    gradient(0)
    arrive(ND + 1)
    gradient(1)
    repack(ND + 3)
    lora(3)
    unpack(0)
    held[...] = rank_rows(dn_v, OUT, (ND, ND + 1))
    unpack(1)
    frozen()
    arrive(ND + 2)
    gradient(2)
    held[...] += rank_rows(dn_v, OUT, (ND + 2,))
    unpack(2)
    arrive(ND + 3)
    sum_start(held[...] + rank_rows(dn_v, OUT, (ND + 3,)), part_u, ring_u, 2)
    unpack(3)
    gradient(3)
    y_wait(ring_u, 2)
    low_u[core, y] = ((ring_u[0] + ring_u[1]) + (ring_u[2] + ring_u[3])).astype(BF)
    for k in range(1, 4):
        t = lax.rem(y + k, 4)
        remote(low_u.at[core, y], low_u.at[core, y], y_s.at[3, t], y_r.at[3, y], narrow=t).start()
    for k in range(4):
        t = lax.rem(y + k, 4)
        remote(
            low_u.at[core, y], low_u.at[core, y], u_s.at[t], u_r.at[y], wide=twin, narrow=t
        ).start()
    finish(0)
    for k, (at, width) in enumerate(OUT):
        to_twin(dgr[k], dgr[k], 3 + ND + k).wait_recv()
        dg_v[:, at : at + width] += dgr[k][...]
    finish(1)
    for k in range(ND):
        to_twin(xt[k], xt[k], 2 + k).wait_recv()
    for k in range(1, 4):
        t = lax.rem(y + k, 4)
        remote(low_u.at[core, t], low_u.at[core, t], y_s.at[3, t], y_r.at[3, t], narrow=t).wait_recv()
    for k in range(4):
        t = lax.rem(y + k, 4)
        remote(
            low_u.at[1 - core, t], low_u.at[1 - core, t], u_s.at[t], u_r.at[t], wide=twin, narrow=t
        ).wait_recv()
    mine, theirs = rank_pairs(low_u.at[core]), rank_pairs(low_u.at[1 - core])
    for t in range(4):
        part_of = slice(t * PACK, (t + 1) * PACK)
        wide_mask = jnp.where(core == 0, mask[t, :, :512], mask[t, :, 512:])
        spread_u[0, part_of, :] = jnp.concatenate([mine[part_of]] * 4, axis=1) * wide_mask
        spread_u[1, part_of, :] = jnp.concatenate([theirs[part_of]] * 4, axis=1) * mask_t[t]
    for k, (at, width) in enumerate(GRAD):
        both = tn(spread_u[0], xr[k][...].reshape(ROWS, width))
        both = both + tn(spread_u[1], xt[k][...].reshape(ROWS, width))
        ug_v[:, at : at + width] += adapter_scale * both
    for k in range(2, len(BACK) - 1):
        finish(k)
    z_sent(zs_c, zc_s, zc_r)
    x_sent(xs_c, xc_s, xc_r)
    for k in range(len(OUT) + ND):
        z_sent(zs[k], z_s.at[k], z_r.at[k])
        x_sent(xs[k], x_s.at[k], x_r.at[k])
    for k in range(len(OUT)):
        to_twin(dgs[k], dgs[k], 3 + ND + k).wait_send()
    for k in range(ND):
        to_twin(xr[k], xr[k], 2 + k).wait_send()
    to_twin(xr_c, xr_c, 2 + ND).wait_send()
    for k in range(len(BACK)):
        if k < len(BACK) - 1:
            z_sent(zs_l[k], zl_s.at[k], zl_r.at[k])
        x_sent(ls[k], xl_s.at[k], xl_r.at[k])
    to_twin(up_v.at[core], up_v.at[core], 0).wait_send()
    to_twin(dn_v.at[core], dn_v.at[core], 1).wait_send()
    for k in range(4):
        t = lax.rem(y + k, 4)
        remote(low_u.at[0, t], low_u.at[0, t], u_s.at[t], u_r.at[t], wide=twin, narrow=t).wait_send()
    for n, buf in enumerate((ring, low, ring_u, low_u.at[0], cot_v, w_v)):
        for k in range(1, 4):
            t = lax.rem(y + k, 4)
            remote(buf.at[t], buf.at[t], y_s.at[n, t], y_r.at[n, t], narrow=t).wait_send()
    finish(len(BACK) - 1)
    z_sent(zs_l[len(BACK) - 1], zl_s.at[len(BACK) - 1], zl_r.at[len(BACK) - 1])


def deliver(*refs):
    nb = len(BACK)
    *lig, dg, ug = refs[: nb + 2]
    lig_out, dg_out, ug_out, sem = refs[nb + 2 :]
    copies = [pltpu.make_async_copy(dg, dg_out, sem.at[nb]), pltpu.make_async_copy(ug, ug_out, sem.at[nb + 1])]
    for k, (at, width) in enumerate(BACK):
        copies.append(pltpu.make_async_copy(lig[k], lig_out.at[:, pl.ds(at, width)], sem.at[k]))
    for c in copies:
        c.start()
    for c in copies:
        c.wait()


def on_device(
    tokens,
    cotangent,
    frozen_key_weight,
    adapter_down_maps,
    adapter_up_maps,
    previous_down_maps,
    previous_up_maps,
    down_fisher_diagonal,
    up_fisher_diagonal,
    token_adapter_index,
):
    vmem = pltpu.VMEM
    dma = pltpu.SemaphoreType.DMA
    no, nb = len(OUT) + ND, len(BACK)
    RANKED = GRAD + OUT
    each = lambda chunks, dims, kind: tuple(vmem((*dims, width), kind) for _, width in chunks)
    scratch = [
        vmem((1, 512), jnp.int32), vmem((512, 1024), BF), vmem((4, 512, 256), BF), vmem((4, 1024, 256), BF),
        vmem((2, 512, 1024), BF), vmem((2, 512, 256), BF), vmem((512, 1024), BF), vmem((512, 256), BF),
        vmem((512, 1024), F32), vmem((512, 256), F32),
        vmem((512, 1024), F32),
        vmem((ZALL, 512), BF), vmem((512, ZALL), BF), vmem((ROWS, ZALL), BF), vmem((ZALL, ROWS), BF),
        each(RANKED, (8, ZROWS), BF), each(RANKED, (8, ZROWS), BF),
        vmem((8, 1, 128), F32), vmem((8, 1, 128), F32),
        each(RANKED, (4, PACK), BF), each(RANKED, (4, PACK), BF),
        vmem((4, 16, 384), BF), vmem((4, 16, 384), BF),
        each(BACK, (4, PACK), BF), each(BACK, (4, PACK), BF),
        each(BACK, (8, ZROWS), BF), each(BACK, (8, ZROWS), BF),
        vmem((4, PACK, 1024), BF), vmem((2, ROWS, 512), BF), vmem((2, ROWS, 512), BF),
        vmem((4, QUARTER, 128), F32), vmem((4, QUARTER, 128), F32), vmem((4, QUARTER, 128), BF),
        vmem((4, QUARTER, 128), F32), vmem((4, QUARTER, 128), F32), vmem((2, 4, QUARTER, 128), BF),
        each(OUT, (512,), F32), each(OUT, (512,), F32),
        vmem((ROWS, 128), F32), each(GRAD, (4, PACK), BF), vmem((4, 16, 384), BF), vmem((4, PACK, 512), BF),
        dma((12 + nb,)), dma((no, 8)), dma((no, 8)), dma((8,)), dma((8,)), dma((nb, 8)), dma((nb, 8)),
        dma((no, 4)), dma((no, 4)), dma((4,)), dma((4,)), dma((nb, 4)), dma((nb, 4)),
        dma((6, 4)), dma((6, 4)), dma((3 + no,)), dma((3 + no,)), dma((4,)), dma((4,)),
    ]
    flat = lambda a: a.reshape(512, -1)
    *lig, dg, ug = pl.pallas_call(
        kernel,
        out_shape=(
            *(pltpu.VMEM((512, width), BF) for _, width in BACK),
            pltpu.VMEM((512, 1024), F32),
            pltpu.VMEM((512, 256), F32),
        ),
        in_specs=[pl.BlockSpec(memory_space=pl.ANY)] * 10,
        out_specs=[pl.BlockSpec(memory_space=pltpu.VMEM)] * (nb + 2),
        scratch_shapes=scratch,
        compiler_params=pltpu.CompilerParams(
            collective_id=0, has_side_effects=True, vmem_limit_bytes=56 * 1024 * 1024
        ),
        cost_estimate=pl.CostEstimate(flops=12_000_000_000, bytes_accessed=12_000_000, transcendentals=0),
    )(
        token_adapter_index.reshape(1, 512),
        tokens,
        cotangent,
        frozen_key_weight,
        flat(adapter_down_maps),
        flat(adapter_up_maps),
        flat(previous_down_maps),
        flat(previous_up_maps),
        flat(down_fisher_diagonal),
        flat(up_fisher_diagonal),
    )
    lig, dg, ug = pl.pallas_call(
        deliver,
        out_shape=(
            jax.ShapeDtypeStruct((512, 1024), BF),
            jax.ShapeDtypeStruct((512, 1024), F32),
            jax.ShapeDtypeStruct((512, 256), F32),
        ),
        in_specs=[pl.BlockSpec(memory_space=pltpu.VMEM)] * (nb + 2),
        out_specs=[pl.BlockSpec(memory_space=pl.ANY)] * 3,
        scratch_shapes=[dma((nb + 2,))],
        compiler_params=pltpu.CompilerParams(vmem_limit_bytes=1024 * 1024),
        cost_estimate=pl.CostEstimate(flops=0, bytes_accessed=7_340_032, transcendentals=0),
    )(*(pltpu.with_memory_space_constraint(a, pltpu.VMEM) for a in (*lig, dg, ug)))
    return lig, dg.reshape(adapter_down_maps.shape), ug.reshape(adapter_up_maps.shape)


def solution(mesh):
    in_specs = (
        P("wide", "narrow"),
        P("wide", "narrow"),
        P(None, "narrow"),
        P("wide", None, "narrow"),
        P("wide", None, "narrow"),
        P("wide", None, "narrow"),
        P("wide", None, "narrow"),
        P("wide", None, "narrow"),
        P("wide", None, "narrow"),
        P("wide"),
    )
    out_specs = (P("wide", "narrow"), P("wide", None, "narrow"), P("wide", None, "narrow"))
    return jax.shard_map(
        on_device, mesh=mesh, in_specs=in_specs, out_specs=out_specs, check_vma=False
    )
```

```python
import jax
import jax.numpy as jnp
from jax import lax
from jax.experimental import pallas as pl
from jax.experimental.pallas import tpu as pltpu
from jax.sharding import PartitionSpec as P

MESH = pl.DeviceIdType.MESH
BF = jnp.bfloat16
F32 = jnp.float32

adapter_scale = 2.0
anchor_penalty_weight = 20.0

OFFSET = (1, 7, 2, 6, 3, 5, 4, 0)
MIRROR = (1, 0, 3, 2, 5, 4, 6, 7)
OWN = 7
ZROWS = 96
ZALL = 8 * ZROWS
SLOTS = 34
PACK = 8 * SLOTS
ROWS = 4 * PACK
HALF = 576
QUARTER = 144
COLS = 256
GRAD = ((0, 128), (128, 128))
ND = len(GRAD)
OUT = ((0, 256), (256, 256), (512, 256), (768, 256))
BACK = ((0, 256), (256, 256), (512, 256), (768, 256))


def iota(shape, dim):
    return lax.broadcasted_iota(jnp.int32, shape, dim)


def fiota(shape, dim):
    return iota(shape, dim).astype(F32)


def onehot(hit):
    return jnp.where(hit, 1.0, 0.0).astype(BF)


def nn(a, b):
    return jnp.dot(a, b, preferred_element_type=F32)


def nt(a, b):
    return lax.dot_general(a, b, (((1,), (1,)), ((), ())), preferred_element_type=F32)


def tn(a, b):
    return lax.dot_general(a, b, (((0,), (0,)), ((), ())), preferred_element_type=F32)


def remote(src, dst, send, recv, **where):
    return pltpu.make_async_remote_copy(
        src_ref=src, dst_ref=dst, send_sem=send, recv_sem=recv, device_id=where, device_id_type=MESH
    )


def offset_at(block):
    half = block >> 1
    return jnp.where(block == OWN, 0, jnp.where((block & 1) == 0, half + 1, 7 - half))


def kernel(
    idx_h, tok_h, cot_h, w_h, dn_h, up_h, pdn_h, pup_h, fd_h, fu_h,
    lig_0, lig_1, lig_2, lig_3, dg_v, ug_v,
    idx_v, tok_v, cot_v, w_v, dn_v, up_v, pdn_v, pup_v, fd_v, fu_v,
    acc,
    g_mat, gt_mat, p_mat, pt_mat,
    zs, zr, zs_c, zr_c, xs, xr, xs_c, xr_c, ls, lr, zs_l, zr_l,
    mask, spread, spread_u, part, ring, low, part_u, ring_u, low_u,
    dgs, dgr, held, xt, xt_c, mask_t,
    loc, z_s, z_r, zc_s, zc_r, zl_s, zl_r, x_s, x_r, xc_s, xc_r, xl_s, xl_r, y_s, y_r, c_s, c_r, u_s, u_r,
):
    lig_v = (lig_0, lig_1, lig_2, lig_3)
    wide = lax.axis_index("wide")
    y = lax.axis_index("narrow")
    z = wide // 8
    me = wide % 8
    x = me // 2
    core = me % 2
    twin = wide + 1 - 2 * core

    def z_dev(offset):
        return lax.rem(z + offset, 8) * 8 + me

    def x_at(k):
        return lax.rem(x + k, 4)

    def x_dev(t):
        return z * 8 + t * 2 + core

    bar = pltpu.get_barrier_semaphore()
    for k in range(1, 8):
        pl.semaphore_signal(bar, inc=1, device_id={"wide": z_dev(k)}, device_id_type=MESH)
    for k in range(1, 4):
        pl.semaphore_signal(bar, inc=1, device_id={"wide": x_dev(x_at(k))}, device_id_type=MESH)
        t = lax.rem(y + k, 4)
        pl.semaphore_signal(bar, inc=1, device_id={"narrow": t}, device_id_type=MESH)
        pl.semaphore_signal(bar, inc=1, device_id={"wide": twin, "narrow": t}, device_id_type=MESH)
    pl.semaphore_signal(bar, inc=1, device_id={"wide": twin}, device_id_type=MESH)

    local = [
        pltpu.make_async_copy(a, b, loc.at[i])
        for i, (a, b) in enumerate(
            [
                (idx_h, idx_v), (cot_h, cot_v.at[y]), (tok_h, tok_v), (up_h, up_v.at[core]), (dn_h, dn_v.at[core]),
                (w_h.at[pl.ds(pl.multiple_of(y * 1024, 1024), 1024)], w_v.at[y]),
                (pdn_h, pdn_v), (pup_h, pup_v), (fd_h, fd_v), (fu_h, fu_v),
            ]
        )
    ]
    for c in local:
        c.start()

    local[0].wait()
    hi = idx_v[...] >> 6
    code = ((idx_v[...] & 63) + 1).astype(F32)
    row = iota((8, 512), 0)
    hit = ((z + offset_at(row)) & 7) == hi
    rank = nn(onehot(hit), onehot(iota((512, 512), 0) < iota((512, 512), 1)))
    slot = jnp.sum(jnp.where(hit, rank + row.astype(F32) * ZROWS, 0.0), axis=0, keepdims=True)
    g_mat[...] = onehot(slot == fiota((ZALL, 512), 0))
    code16 = jnp.broadcast_to(code, (16, 512)).astype(BF)
    for b in range(8):
        sent = nt(code16, g_mat[b * ZROWS : (b + 1) * ZROWS, :])[:1]
        zs_c[b] = jnp.concatenate([sent, jnp.zeros((1, 128 - ZROWS), F32)], axis=1)
    local[1].wait()
    for k, (at, width) in enumerate(GRAD):
        packed = nn(g_mat[...], cot_v[y, :, at : at + width])
        zs[k][...] = packed.astype(BF).reshape(8, ZROWS, width)

    pl.semaphore_wait(bar, 17)

    def z_copy(src, dst, send, recv, b):
        return remote(src.at[b], dst.at[MIRROR[b]], send.at[b], recv.at[MIRROR[b]], wide=z_dev(OFFSET[b]))

    def z_start(src, dst, send, recv):
        for b in range(7):
            z_copy(src, dst, send, recv, b).start()
        dst[OWN] = src[OWN]

    def z_wait(dst, send, recv):
        for b in range(7):
            remote(dst.at[b], dst.at[b], send.at[b], recv.at[b], wide=z_dev(OFFSET[b])).wait_recv()

    def z_sent(src, send, recv):
        for b in range(7):
            remote(src.at[b], src.at[b], send.at[b], recv.at[b], wide=z_dev(OFFSET[b])).wait_send()

    def x_start(src, dst, send, recv):
        for k in range(1, 4):
            t = x_at(k)
            remote(src.at[t], dst.at[x], send.at[t], recv.at[x], wide=x_dev(t)).start()
        dst[x] = src[x]

    def x_wait(dst, send, recv):
        for k in range(1, 4):
            t = x_at(k)
            remote(dst.at[t], dst.at[t], send.at[t], recv.at[t], wide=x_dev(t)).wait_recv()

    def x_sent(src, send, recv):
        for k in range(1, 4):
            t = x_at(k)
            remote(src.at[t], src.at[t], send.at[t], recv.at[t], wide=x_dev(t)).wait_send()

    def to_twin(src, dst, n):
        return remote(src, dst, c_s.at[n], c_r.at[n], wide=twin)

    z_start(zs_c, zr_c, zc_s, zc_r)
    for k in range(ND):
        z_start(zs[k], zr[k], z_s.at[k], z_r.at[k])
    local[3].wait()
    local[4].wait()
    to_twin(up_v.at[core], up_v.at[core], 0).start()
    to_twin(dn_v.at[core], dn_v.at[core], 1).start()

    def y_share(buf, n):
        for k in range(1, 4):
            t = lax.rem(y + k, 4)
            remote(buf.at[y], buf.at[y], y_s.at[n, t], y_r.at[n, y], narrow=t).start()

    def y_wait(dst, n):
        for k in range(1, 4):
            t = lax.rem(y + k, 4)
            remote(dst.at[t], dst.at[t], y_s.at[n, t], y_r.at[n, t], narrow=t).wait_recv()

    y_share(cot_v, 4)
    local[2].wait()
    for k, (at, width) in enumerate(OUT, ND):
        packed = nn(g_mat[...], tok_v[:, at : at + width])
        zs[k][...] = packed.astype(BF).reshape(8, ZROWS, width)
        z_start(zs[k], zr[k], z_s.at[k], z_r.at[k])

    z_wait(zr_c, zc_s, zc_r)
    codes = zr_c[:, 0, :]
    upper = onehot(iota((128, 128), 0) < iota((128, 128), 1))
    place = jnp.zeros((8, 128), F32)
    for t in range(4):
        inside = (codes > 16.0 * t) & (codes < 16.0 * t + 17.0)
        spot = nn(onehot(inside), upper) + fiota((8, 128), 0) * SLOTS + float(t * PACK + 1)
        place = place + jnp.where(inside, spot, 0.0)
    place = jnp.concatenate([place[m : m + 1, :ZROWS] for m in range(8)], axis=1) - 1.0
    p_mat[...] = onehot(place == fiota((ROWS, ZALL), 0))
    line = jnp.concatenate([codes[m : m + 1, :ZROWS] for m in range(8)], axis=1)
    line = jnp.broadcast_to(line, (16, ZALL)).astype(BF)
    for t in range(4):
        sent = nt(line, p_mat[t * PACK : (t + 1) * PACK, :])
        xs_c[t] = jnp.concatenate([sent, jnp.zeros((16, 384 - PACK), F32)], axis=1).astype(BF)
    x_start(xs_c, xr_c, xc_s, xc_r)

    def repack(k):
        width = zr[k].shape[2]
        z_wait(zr[k], z_s.at[k], z_r.at[k])
        rows = nn(p_mat[...], zr[k][...].reshape(ZALL, width))
        xs[k][...] = rows.astype(BF).reshape(4, PACK, width)
        x_start(xs[k], xr[k], x_s.at[k], x_r.at[k])

    for k in range(ND):
        repack(k)

    codes32 = jnp.concatenate([jnp.broadcast_to(codes[m : m + 1], (4, 128)) for m in range(8)], axis=0)
    col = nt(onehot(iota((ZROWS, 128), 0) == iota((ZROWS, 128), 1)), codes32.astype(BF))
    lane = iota((ZROWS, 32), 1)
    first = (lane & 3).astype(F32) * 16.0
    inside = (col > first) & (col < first + 17.0)
    spot = nn(onehot(iota((ZROWS, ZROWS), 0) > iota((ZROWS, ZROWS), 1)), onehot(inside))
    spot = spot + ((lane & 3) * PACK + (lane >> 2) * SLOTS + 1).astype(F32)
    for m in range(8):
        at = jnp.sum(jnp.where(inside & ((lane >> 2) == m), spot, 0.0), axis=1, keepdims=True) - 1.0
        pt_mat[m * ZROWS : (m + 1) * ZROWS, :] = onehot(at == fiota((ZROWS, ROWS), 1))

    def named(codes, t, lanes, base):
        seen = nt(onehot(iota((PACK, 384), 0) == iota((PACK, 384), 1)), codes[t])[:, :1]
        return onehot(seen == (iota((PACK, lanes), 1) // 64 + base).astype(F32))

    x_wait(xr_c, xc_s, xc_r)
    for t in range(4):
        mask[t] = named(xr_c, t, 1024, 1 + 16 * x)

    def fold(every, t):
        kept = every * mask[t].astype(F32)
        total = kept[:, :128]
        for j in range(1, 8):
            total = total + kept[:, j * 128 : (j + 1) * 128]
        return total + pltpu.roll(total, 64, 1)

    left = iota((HALF, 128), 1) < 64

    def arrive(k):
        x_wait(xr[k], x_s.at[k], x_r.at[k])

    def rank_rows(maps, chunks, ks):
        sums = []
        for t in range(4):
            every = None
            for k in ks:
                at, width = chunks[k] if chunks is GRAD else chunks[k - ND]
                one = nt(xr[k][t], maps[:, :, at : at + width].reshape(1024, width))
                every = one if every is None else every + one
            sums.append(fold(every, t))
        return jnp.concatenate(sums, axis=0)

    def sum_start(rows, source, dst, n):
        lower = jnp.concatenate([rows[HALF:], jnp.zeros((2 * HALF - ROWS, 128), F32)], axis=0)
        source[...] = jnp.where(left, rows[:HALF], lower).reshape(4, QUARTER, 128)
        for k in range(1, 4):
            t = lax.rem(y + k, 4)
            remote(source.at[t], dst.at[y], y_s.at[n, t], y_r.at[n, y], narrow=t).start()
        dst[y] = source[y]

    def sum_share(src, dst, n):
        y_wait(src, n)
        dst[y] = ((src[0] + src[1]) + (src[2] + src[3])).astype(BF)
        y_share(dst, n + 1)

    def rank_pairs(buf):
        value = buf[...].reshape(HALF, 128).astype(F32)
        other = pltpu.roll(value, 64, 1)
        high = jnp.where(left, value, other).astype(BF)
        rest = jnp.where(left, other, value).astype(BF)
        return jnp.concatenate([high, rest[: ROWS - HALF]], axis=0)

    def spread_of(buf, out):
        both = rank_pairs(buf)
        for t in range(4):
            one = jnp.concatenate([both[t * PACK : (t + 1) * PACK]] * 4, axis=1)
            for c in range(2):
                out[c, t * PACK : (t + 1) * PACK, :] = one * mask[t, :, c * 512 : (c + 1) * 512]

    to_twin(up_v.at[1 - core], up_v.at[1 - core], 0).wait_recv()
    repack(ND)
    for k in range(ND):
        arrive(k)
    sum_start(rank_rows(up_v, GRAD, range(ND)), part, ring, 0)
    for k in range(ND):
        to_twin(xr[k], xt[k], 2 + k).start()
    to_twin(xr_c, xt_c, 2 + ND).start()
    sum_share(ring, low, 0)
    repack(ND + 1)
    for k in range(1, 4):
        t = lax.rem(y + k, 4)
        remote(
            w_h.at[pl.ds(pl.multiple_of(t * 1024, 1024), 1024)],
            w_v.at[y], y_s.at[5, t], y_r.at[5, y], narrow=t,
        ).start()
    def penalties():
        for i in range(6, 10):
            local[i].wait()

        def down(i, carry):
            at = pl.ds(pl.multiple_of(i * 64, 64), 64)
            delta = dn_v[core, at, :].astype(F32) - pdn_v[at, :].astype(F32)
            dg_v[at, :] = anchor_penalty_weight * fd_v[at, :] * delta
            return carry

        lax.fori_loop(0, 8, down, 0)
        delta = up_v[core].astype(F32) - pup_v[...].astype(F32)
        ug_v[...] = anchor_penalty_weight * fu_v[...] * delta

    def return_map():
        hi16 = jnp.broadcast_to(hi, (16, 512)).astype(F32).astype(BF)
        hi_col = nt(onehot(iota((512, 512), 0) == iota((512, 512), 1)), hi16)[:, :1]
        lane = iota((512, 128), 1)
        hit = (((z + offset_at(lane)) & 7).astype(F32) == hi_col) & (lane < 8)
        rank = nn(onehot(iota((512, 512), 0) > iota((512, 512), 1)), onehot(hit))
        slot_col = jnp.where(hit, rank + lane.astype(F32) * ZROWS, 0.0)
        slot_col = jnp.sum(slot_col, axis=1, keepdims=True)
        gt_mat[...] = onehot(slot_col == fiota((512, ZALL), 1))

    penalties()
    return_map()
    to_twin(xt_c, xt_c, 2 + ND).wait_recv()
    for t in range(4):
        mask_t[t] = named(xt_c, t, 512, 1 + 16 * x + 8 * core)
    to_twin(dn_v.at[1 - core], dn_v.at[1 - core], 1).wait_recv()
    y_wait(low, 1)
    spread_of(low, spread)

    def lora(k):
        at, width = BACK[k]
        rows = nn(spread[0], dn_v[0, :, at : at + width])
        rows = rows + nn(spread[1], dn_v[1, :, at : at + width])
        ls[k][...] = (adapter_scale * rows).astype(BF).reshape(4, PACK, width)
        x_start(ls[k], lr[k], xl_s.at[k], xl_r.at[k])

    def unpack(k):
        width = BACK[k][1]
        x_wait(lr[k], xl_s.at[k], xl_r.at[k])
        rows = nn(pt_mat[...], lr[k][...].reshape(ROWS, width)).astype(BF)
        zs_l[k][...] = rows.reshape(8, ZROWS, width)
        z_start(zs_l[k], zr_l[k], zl_s.at[k], zl_r.at[k])

    def gradient(k):
        at, width = OUT[k]
        rows = xr[ND + k][...].reshape(ROWS, width)
        dgs[k][...] = adapter_scale * tn(spread[1 - core], rows)
        to_twin(dgs[k], dgr[k], 3 + ND + k).start()
        dg_v[:, at : at + width] += adapter_scale * tn(spread[core], rows)

    def frozen():
        y_wait(cot_v, 4)
        local[5].wait()
        y_wait(w_v, 5)

        def one(i, carry):
            at = pl.ds(pl.multiple_of(i * 128, 128), 128)
            total = nt(cot_v[0, at, :], w_v[0])
            for j in range(1, 4):
                total = total + nt(cot_v[j, at, :], w_v[j])
            acc[at, :] = total
            return carry

        lax.fori_loop(0, 4, one, 0)


    def finish(k):
        at, width = BACK[k]
        z_wait(zr_l[k], zl_s.at[k], zl_r.at[k])
        back = nn(gt_mat[...], zr_l[k][...].reshape(ZALL, width))
        lig_v[k][...] = (acc[:, at : at + width] + back).astype(BF)

    lora(0)
    lora(1)
    repack(ND + 2)
    lora(2)
    arrive(ND + 0)
    gradient(0)
    arrive(ND + 1)
    gradient(1)
    repack(ND + 3)
    lora(3)
    unpack(0)
    held[...] = rank_rows(dn_v, OUT, (ND, ND + 1))
    unpack(1)
    arrive(ND + 2)
    gradient(2)
    unpack(2)
    frozen()
    held[...] += rank_rows(dn_v, OUT, (ND + 2,))
    arrive(ND + 3)
    sum_start(held[...] + rank_rows(dn_v, OUT, (ND + 3,)), part_u, ring_u, 2)
    unpack(3)
    gradient(3)
    y_wait(ring_u, 2)
    low_u[core, y] = ((ring_u[0] + ring_u[1]) + (ring_u[2] + ring_u[3])).astype(BF)
    for k in range(1, 4):
        t = lax.rem(y + k, 4)
        remote(low_u.at[core, y], low_u.at[core, y], y_s.at[3, t], y_r.at[3, y], narrow=t).start()
    for k in range(4):
        t = lax.rem(y + k, 4)
        remote(
            low_u.at[core, y], low_u.at[core, y], u_s.at[t], u_r.at[y], wide=twin, narrow=t
        ).start()
    finish(0)
    for k, (at, width) in enumerate(OUT):
        to_twin(dgr[k], dgr[k], 3 + ND + k).wait_recv()
        dg_v[:, at : at + width] += dgr[k][...]
    finish(1)
    for k in range(ND):
        to_twin(xt[k], xt[k], 2 + k).wait_recv()
    for k in range(1, 4):
        t = lax.rem(y + k, 4)
        remote(low_u.at[core, t], low_u.at[core, t], y_s.at[3, t], y_r.at[3, t], narrow=t).wait_recv()
    for k in range(4):
        t = lax.rem(y + k, 4)
        remote(
            low_u.at[1 - core, t], low_u.at[1 - core, t], u_s.at[t], u_r.at[t], wide=twin, narrow=t
        ).wait_recv()
    mine, theirs = rank_pairs(low_u.at[core]), rank_pairs(low_u.at[1 - core])
    for t in range(4):
        part_of = slice(t * PACK, (t + 1) * PACK)
        wide_mask = jnp.where(core == 0, mask[t, :, :512], mask[t, :, 512:])
        spread_u[0, part_of, :] = jnp.concatenate([mine[part_of]] * 4, axis=1) * wide_mask
        spread_u[1, part_of, :] = jnp.concatenate([theirs[part_of]] * 4, axis=1) * mask_t[t]
    for k, (at, width) in enumerate(GRAD):
        both = tn(spread_u[0], xr[k][...].reshape(ROWS, width))
        both = both + tn(spread_u[1], xt[k][...].reshape(ROWS, width))
        ug_v[:, at : at + width] += adapter_scale * both
    for k in range(2, len(BACK) - 1):
        finish(k)
    z_sent(zs_c, zc_s, zc_r)
    x_sent(xs_c, xc_s, xc_r)
    for k in range(len(OUT) + ND):
        z_sent(zs[k], z_s.at[k], z_r.at[k])
        x_sent(xs[k], x_s.at[k], x_r.at[k])
    for k in range(len(OUT)):
        to_twin(dgs[k], dgs[k], 3 + ND + k).wait_send()
    for k in range(ND):
        to_twin(xr[k], xr[k], 2 + k).wait_send()
    to_twin(xr_c, xr_c, 2 + ND).wait_send()
    for k in range(len(BACK)):
        if k < len(BACK) - 1:
            z_sent(zs_l[k], zl_s.at[k], zl_r.at[k])
        x_sent(ls[k], xl_s.at[k], xl_r.at[k])
    to_twin(up_v.at[core], up_v.at[core], 0).wait_send()
    to_twin(dn_v.at[core], dn_v.at[core], 1).wait_send()
    for k in range(4):
        t = lax.rem(y + k, 4)
        remote(low_u.at[0, t], low_u.at[0, t], u_s.at[t], u_r.at[t], wide=twin, narrow=t).wait_send()
    for n, buf in enumerate((ring, low, ring_u, low_u.at[0], cot_v, w_v)):
        for k in range(1, 4):
            t = lax.rem(y + k, 4)
            remote(buf.at[t], buf.at[t], y_s.at[n, t], y_r.at[n, t], narrow=t).wait_send()
    finish(len(BACK) - 1)
    z_sent(zs_l[len(BACK) - 1], zl_s.at[len(BACK) - 1], zl_r.at[len(BACK) - 1])


def deliver(*refs):
    nb = len(BACK)
    *lig, dg, ug = refs[: nb + 2]
    lig_out, dg_out, ug_out, sem = refs[nb + 2 :]
    copies = [pltpu.make_async_copy(dg, dg_out, sem.at[nb]), pltpu.make_async_copy(ug, ug_out, sem.at[nb + 1])]
    for k, (at, width) in enumerate(BACK):
        copies.append(pltpu.make_async_copy(lig[k], lig_out.at[:, pl.ds(at, width)], sem.at[k]))
    for c in copies:
        c.start()
    for c in copies:
        c.wait()


def on_device(
    tokens,
    cotangent,
    frozen_key_weight,
    adapter_down_maps,
    adapter_up_maps,
    previous_down_maps,
    previous_up_maps,
    down_fisher_diagonal,
    up_fisher_diagonal,
    token_adapter_index,
):
    vmem = pltpu.VMEM
    dma = pltpu.SemaphoreType.DMA
    no, nb = len(OUT) + ND, len(BACK)
    RANKED = GRAD + OUT
    each = lambda chunks, dims, kind: tuple(vmem((*dims, width), kind) for _, width in chunks)
    scratch = [
        vmem((1, 512), jnp.int32), vmem((512, 1024), BF), vmem((4, 512, 256), BF), vmem((4, 1024, 256), BF),
        vmem((2, 512, 1024), BF), vmem((2, 512, 256), BF), vmem((512, 1024), BF), vmem((512, 256), BF),
        vmem((512, 1024), F32), vmem((512, 256), F32),
        vmem((512, 1024), F32),
        vmem((ZALL, 512), BF), vmem((512, ZALL), BF), vmem((ROWS, ZALL), BF), vmem((ZALL, ROWS), BF),
        each(RANKED, (8, ZROWS), BF), each(RANKED, (8, ZROWS), BF),
        vmem((8, 1, 128), F32), vmem((8, 1, 128), F32),
        each(RANKED, (4, PACK), BF), each(RANKED, (4, PACK), BF),
        vmem((4, 16, 384), BF), vmem((4, 16, 384), BF),
        each(BACK, (4, PACK), BF), each(BACK, (4, PACK), BF),
        each(BACK, (8, ZROWS), BF), each(BACK, (8, ZROWS), BF),
        vmem((4, PACK, 1024), BF), vmem((2, ROWS, 512), BF), vmem((2, ROWS, 512), BF),
        vmem((4, QUARTER, 128), F32), vmem((4, QUARTER, 128), F32), vmem((4, QUARTER, 128), BF),
        vmem((4, QUARTER, 128), F32), vmem((4, QUARTER, 128), F32), vmem((2, 4, QUARTER, 128), BF),
        each(OUT, (512,), F32), each(OUT, (512,), F32),
        vmem((ROWS, 128), F32), each(GRAD, (4, PACK), BF), vmem((4, 16, 384), BF), vmem((4, PACK, 512), BF),
        dma((12 + nb,)), dma((no, 8)), dma((no, 8)), dma((8,)), dma((8,)), dma((nb, 8)), dma((nb, 8)),
        dma((no, 4)), dma((no, 4)), dma((4,)), dma((4,)), dma((nb, 4)), dma((nb, 4)),
        dma((6, 4)), dma((6, 4)), dma((3 + no,)), dma((3 + no,)), dma((4,)), dma((4,)),
    ]
    flat = lambda a: a.reshape(512, -1)
    *lig, dg, ug = pl.pallas_call(
        kernel,
        out_shape=(
            *(pltpu.VMEM((512, width), BF) for _, width in BACK),
            pltpu.VMEM((512, 1024), F32),
            pltpu.VMEM((512, 256), F32),
        ),
        in_specs=[pl.BlockSpec(memory_space=pl.ANY)] * 10,
        out_specs=[pl.BlockSpec(memory_space=pltpu.VMEM)] * (nb + 2),
        scratch_shapes=scratch,
        compiler_params=pltpu.CompilerParams(
            collective_id=0, has_side_effects=True, vmem_limit_bytes=56 * 1024 * 1024
        ),
        cost_estimate=pl.CostEstimate(flops=12_000_000_000, bytes_accessed=12_000_000, transcendentals=0),
    )(
        token_adapter_index.reshape(1, 512),
        tokens,
        cotangent,
        frozen_key_weight,
        flat(adapter_down_maps),
        flat(adapter_up_maps),
        flat(previous_down_maps),
        flat(previous_up_maps),
        flat(down_fisher_diagonal),
        flat(up_fisher_diagonal),
    )
    lig, dg, ug = pl.pallas_call(
        deliver,
        out_shape=(
            jax.ShapeDtypeStruct((512, 1024), BF),
            jax.ShapeDtypeStruct((512, 1024), F32),
            jax.ShapeDtypeStruct((512, 256), F32),
        ),
        in_specs=[pl.BlockSpec(memory_space=pltpu.VMEM)] * (nb + 2),
        out_specs=[pl.BlockSpec(memory_space=pl.ANY)] * 3,
        scratch_shapes=[dma((nb + 2,))],
        compiler_params=pltpu.CompilerParams(vmem_limit_bytes=1024 * 1024),
        cost_estimate=pl.CostEstimate(flops=0, bytes_accessed=7_340_032, transcendentals=0),
    )(*(pltpu.with_memory_space_constraint(a, pltpu.VMEM) for a in (*lig, dg, ug)))
    return lig, dg.reshape(adapter_down_maps.shape), ug.reshape(adapter_up_maps.shape)


def solution(mesh):
    in_specs = (
        P("wide", "narrow"),
        P("wide", "narrow"),
        P(None, "narrow"),
        P("wide", None, "narrow"),
        P("wide", None, "narrow"),
        P("wide", None, "narrow"),
        P("wide", None, "narrow"),
        P("wide", None, "narrow"),
        P("wide", None, "narrow"),
        P("wide"),
    )
    out_specs = (P("wide", "narrow"), P("wide", None, "narrow"), P("wide", None, "narrow"))
    return jax.shard_map(
        on_device, mesh=mesh, in_specs=in_specs, out_specs=out_specs, check_vma=False
    )
```
